512 devices in a mesh: seq: 128 (over y, z, core), head: 4 (over x).
Axes of the slice: x: 4, y: 8, z: 8, core: 2. Of those that a mesh axis runs over, the one named last changes fastest.
Arguments:
- queries: bfloat16 [32768, 1024], P('seq', 'head'), may hold values from -5 to 5
- keys: bfloat16 [32768, 1024], P('seq', 'head'), may hold values from -5 to 5
- values: bfloat16 [32768, 1024], P('seq', 'head'), may hold values from -6 to 6
- out_grad: bfloat16 [32768, 1024], P('seq', 'head'), may hold values from -6 to 6
- sorted_position: int32 [2, 32768], P(None, ('seq', 'head')), may hold values from 0 to 32767, as said below
Outputs:
- query_grad: bfloat16 [32768, 1024], P('seq', 'head')
- key_grad: bfloat16 [32768, 1024], P('seq', 'head')
- value_grad: bfloat16 [32768, 1024], P('seq', 'head')
The draws below stay inside these ranges and needn't reach their ends.
Inputs may be any that keep to these rules, and one draw needn't show every extreme that they name: `sorted_position`: each row is a permutation of 0 to 32767. For every round, at most 4 tokens of one block of 256 consecutive tokens take places in one block of 256 consecutive places, and every block of places takes exactly 4 from some block of tokens.
All inputs are finite; a program needn't handle non-finite values.
Results may differ from the reference program's by a relative error of at most 0.025.
Values may be sent and summed in bfloat16 or wider, within the bound.
No kernel may reach another device: no remote copies, remote signals or barrier semaphores. Data moves between devices by JAX's collectives and lax.ppermute only.
A program may use at most 64 MiB of HBM per device.

```python
import math
import jax
import jax.numpy as jnp
from jax import lax

HEADS = 8
HEAD_DIM = 128
ROUNDS = 2
SPAN = 256
TOK_DEV = 256
TOKENS = 32768
CAP = 4
N_SEQ = 128


def bucket_orders(key):
    base = jax.random.fold_in(key, 101)
    orders = []
    places = []
    for turn in range(ROUNDS):
        round_key = jax.random.fold_in(base, turn)
        key_grid, key_owner, key_local, key_tie = jax.random.split(round_key, 4)
        cells = (N_SEQ - 1) * CAP
        picked = jax.random.permutation(key_grid, cells)
        chosen = (jnp.arange(cells) < TOK_DEV - CAP).astype(jnp.int32)
        spread = jnp.zeros((N_SEQ - 1,), jnp.int32).at[picked // CAP].add(chosen)
        profile = jnp.concatenate([jnp.full((1,), CAP, jnp.int32), spread])
        owner_of = jax.random.permutation(key_owner, N_SEQ).astype(jnp.int32)
        source = jnp.arange(N_SEQ, dtype=jnp.int32)[:, None]
        counts = profile[(owner_of[None, :] - source) % N_SEQ]
        bounds = jnp.cumsum(counts, axis=1)
        local = jax.vmap(lambda sub_key: jax.random.permutation(sub_key, TOK_DEV))(jax.random.split(key_local, N_SEQ))
        target = jax.vmap(lambda edge, rank: jnp.searchsorted(edge, rank, side='right'))(bounds, local)
        tie_break = jax.random.permutation(key_tie, TOKENS).astype(jnp.int32)
        score = target.reshape(-1).astype(jnp.int32) * TOKENS + tie_break
        order = jnp.argsort(score).astype(jnp.int32)
        place = jnp.zeros((TOKENS,), jnp.int32).at[order].set(jnp.arange(TOKENS, dtype=jnp.int32))
        orders.append(order)
        places.append(place)
    return jnp.stack(places)


def draw_sorted_position(key, part):
    places = bucket_orders(key)
    return places


def draw_queries(key, part):
    own_key = jax.random.fold_in(key, 3)
    return jnp.clip(jax.random.normal(own_key, (TOKENS, HEADS * HEAD_DIM)), -5.0, 5.0).astype(jnp.bfloat16)


def draw_keys(key, part):
    own_key = jax.random.fold_in(key, 5)
    return jnp.clip(jax.random.normal(own_key, (TOKENS, HEADS * HEAD_DIM)), -5.0, 5.0).astype(jnp.bfloat16)


def block_levels(rng, extent, cuts, low, high):
    def one(axis_at, blocks):
        steps = jax.random.uniform(jax.random.fold_in(jax.random.fold_in(rng, 6), axis_at), (blocks,), jnp.float32, low / len(cuts), high / len(cuts))
        return jnp.repeat(jnp.exp(steps), extent[axis_at] // blocks).reshape((-1,) + (1,) * (len(extent) - axis_at - 1))

    loudness = one(*cuts[0])
    for cut in cuts[1:]:
        loudness = loudness * one(*cut)
    return loudness


def bell_draw(rng, shape, scale, most, pieces=(), kind=jnp.bfloat16):
    result = jax.random.normal(rng, shape, jnp.float32) * scale
    if len(pieces) > 0:
        result = block_levels(rng, shape, pieces, -0.22, 0.18) * result
    return jnp.clip(result, min=-most, max=most).astype(kind)


def setup_inputs(seed: int = 0) -> dict:
    streams_of = jax.random.split(jax.random.key(seed), 6)
    return {
        "queries": draw_queries(jax.random.fold_in(streams_of[5], 71), 0),
        "keys": draw_keys(jax.random.fold_in(streams_of[5], 71), 0),
        "values": bell_draw(streams_of[2], (TOKENS, HEADS * HEAD_DIM), 1.0, 6.0, ((0, 128), (1, 4))),
        "out_grad": bell_draw(streams_of[3], (TOKENS, HEADS * HEAD_DIM), 1.0, 6.0, ((0, 128), (1, 4))),
        "sorted_position": draw_sorted_position(jax.random.fold_in(streams_of[5], 71), 0),
    }


HIGH = lax.Precision.HIGHEST

def span_sets(rows):
    blocks = rows.reshape(-1, SPAN, rows.shape[1])
    return jnp.concatenate([jnp.roll(blocks, 1, axis=0), blocks], axis=1)

def rounded(array):
    return lax.optimization_barrier(array.astype(jnp.bfloat16)).astype(jnp.float32)

def span_attention(q_sorted, k_sorted):
    scale = 1.0 / math.sqrt(HEAD_DIM)
    query_blocks = q_sorted.reshape(-1, SPAN, HEAD_DIM).astype(jnp.float32)
    key_blocks = span_sets(k_sorted).astype(jnp.float32)
    scores = jnp.einsum('nqd,nkd->nqk', query_blocks, key_blocks, precision=HIGH) * scale
    highest = lax.optimization_barrier(jnp.max(scores, axis=2, keepdims=True))
    log_total = highest + jnp.log(lax.optimization_barrier(jnp.sum(jnp.exp(scores - highest), axis=2, keepdims=True)))
    return (jnp.exp(scores - log_total), log_total[:, :, 0])

def head_forward(q_sorted, k_sorted, v_sorted):
    attention, log_total = span_attention(q_sorted, k_sorted)
    value_blocks = span_sets(v_sorted).astype(jnp.float32)
    mixed = jnp.einsum('nqk,nkd->nqd', rounded(attention), value_blocks, precision=HIGH)
    return (log_total.reshape(-1), mixed.reshape(-1, HEAD_DIM).astype(jnp.bfloat16))

def head_backward(q_sorted, k_sorted, v_sorted, g_sorted, o_sorted, share, grad_log):
    scale = 1.0 / math.sqrt(HEAD_DIM)
    attention, log_total = span_attention(q_sorted, k_sorted)
    grad_out = rounded(share[:, None] * g_sorted.astype(jnp.float32))
    delta = lax.optimization_barrier(jnp.sum(grad_out * o_sorted.astype(jnp.float32), axis=1))
    grad_blocks = grad_out.reshape(-1, SPAN, HEAD_DIM)
    query_blocks = q_sorted.reshape(-1, SPAN, HEAD_DIM).astype(jnp.float32)
    key_blocks = span_sets(k_sorted).astype(jnp.float32)
    value_blocks = span_sets(v_sorted).astype(jnp.float32)
    grad_attention = jnp.einsum('nqd,nkd->nqk', grad_blocks, value_blocks, precision=HIGH)
    grad_score = attention * (grad_attention - delta.reshape(-1, SPAN, 1) + grad_log.reshape(-1, SPAN, 1))
    scaled = rounded(grad_score * scale)
    grad_q = jnp.einsum('nqk,nkd->nqd', scaled, key_blocks, precision=HIGH)
    grad_k_sets = jnp.einsum('nqk,nqd->nkd', scaled, query_blocks, precision=HIGH)
    grad_v_sets = jnp.einsum('nqk,nqd->nkd', rounded(attention), grad_blocks, precision=HIGH)
    grad_k = grad_k_sets[:, SPAN:] + jnp.roll(grad_k_sets[:, :SPAN], -1, axis=0)
    grad_v = grad_v_sets[:, SPAN:] + jnp.roll(grad_v_sets[:, :SPAN], -1, axis=0)
    return (grad_q.reshape(-1, HEAD_DIM).astype(jnp.bfloat16), grad_k.reshape(-1, HEAD_DIM).astype(jnp.bfloat16), grad_v.reshape(-1, HEAD_DIM).astype(jnp.bfloat16))

def by_head(array):
    return array.reshape(TOKENS, HEADS, HEAD_DIM).transpose(1, 0, 2)

def reference(queries, keys, values, out_grad, sorted_position):
    heads_q = by_head(queries)
    heads_k = by_head(keys)
    heads_v = by_head(values)
    heads_g = by_head(out_grad)
    orders = [jnp.argsort(sorted_position[turn]).astype(jnp.int32) for turn in range(ROUNDS)]
    outs_sorted = []
    totals = []
    dots = []
    for turn in range(ROUNDS):
        order = orders[turn]
        place = sorted_position[turn].astype(jnp.int32)

        def forward_head(parts, order=order):
            return head_forward(parts[0][order], parts[1][order], parts[2][order])
        total_sorted, out_sorted = lax.map(forward_head, (heads_q, heads_k, heads_v))
        outs_sorted.append(out_sorted)
        totals.append(total_sorted[:, place])
        dots.append(lax.optimization_barrier(jnp.sum(heads_g.astype(jnp.float32) * out_sorted[:, place].astype(jnp.float32), axis=2)))
    total = jnp.stack(totals)
    dot = jnp.stack(dots)
    highest = lax.optimization_barrier(jnp.max(total, axis=0, keepdims=True))
    raised = jnp.exp(total - highest)
    share = raised / lax.optimization_barrier(jnp.sum(raised, axis=0, keepdims=True))
    grad_log = share * (dot - lax.optimization_barrier(jnp.sum(share * dot, axis=0, keepdims=True)))
    sum_q = jnp.zeros((HEADS, TOKENS, HEAD_DIM), jnp.float32)
    sum_k = jnp.zeros((HEADS, TOKENS, HEAD_DIM), jnp.float32)
    sum_v = jnp.zeros((HEADS, TOKENS, HEAD_DIM), jnp.float32)
    for turn in range(ROUNDS):
        order = orders[turn]
        place = sorted_position[turn].astype(jnp.int32)

        def backward_head(parts, order=order):
            return head_backward(parts[0][order], parts[1][order], parts[2][order], parts[3][order], parts[4], parts[5][order], parts[6][order])
        grad_q, grad_k, grad_v = lax.map(backward_head, (heads_q, heads_k, heads_v, heads_g, outs_sorted[turn], share[turn], grad_log[turn]))
        sum_q = sum_q + grad_q[:, place].astype(jnp.float32)
        sum_k = sum_k + grad_k[:, place].astype(jnp.float32)
        sum_v = sum_v + grad_v[:, place].astype(jnp.float32)

    def back_to_rows(array):
        return array.astype(jnp.bfloat16).transpose(1, 0, 2).reshape(TOKENS, HEADS * HEAD_DIM)
    return (back_to_rows(sum_q), back_to_rows(sum_k), back_to_rows(sum_v))
```

```python
import functools
import math

import jax
import jax.numpy as jnp
from jax import lax
from jax.experimental import pallas as pl
from jax.experimental.pallas import tpu as pltpu
from jax.sharding import PartitionSpec as P

HEAD_DIM = 128
SPAN = 256
ROUNDS = 2
CAP = 4
SLOTS = ROUNDS * CAP
LANES = 128
EMPTY = 8.0
SCALE = 1.0 / math.sqrt(HEAD_DIM)
F32 = jnp.float32
BF16 = jnp.bfloat16
I32 = jnp.int32


def iota(shape, dim):
    return lax.broadcasted_iota(I32, shape, dim)


def hot(condition):
    return jnp.where(condition, 1.0, 0.0).astype(BF16)


def dot(a, b):
    return lax.dot_general(a, b, (((1,), (0,)), ((), ())), preferred_element_type=F32)


def dot_nt(a, b):
    return lax.dot_general(a, b, (((1,), (1,)), ((), ())), preferred_element_type=F32)


def dot_tn(a, b):
    return lax.dot_general(a, b, (((0,), (0,)), ((), ())), preferred_element_type=F32)


def three_parts(x):
    high = x.astype(BF16).astype(F32)
    rest = x - high
    middle = rest.astype(BF16).astype(F32)
    return high, middle, (rest - middle).astype(BF16).astype(F32)


def picked(x, onehot, product):
    rows = x.shape[0]
    stacked = jnp.concatenate(three_parts(x), axis=0).astype(BF16)
    out = product(stacked, onehot)
    return out[:rows] + out[rows : 2 * rows] + out[2 * rows :]


def slot_rows(slots_ref, turn):
    slot = slots_ref[turn : turn + 1, :]
    return slot >> 3, slot & 7


def compaction(valid, n):
    before = hot(iota((LANES, LANES), 0) < iota((LANES, LANES), 1))
    lane = iota((8, LANES), 1)
    turn = iota((8, LANES), 0)
    running = jnp.zeros((8, 1), F32)
    pieces = []
    for chunk in range(n * SLOTS // LANES):
        part = valid[:, chunk * LANES : (chunk + 1) * LANES]
        mine = jnp.where((((lane >> 2) & 1) == turn) & part, 1.0, 0.0)
        rank = dot(mine.astype(BF16), before) + running
        running = running + jnp.sum(mine, axis=1, keepdims=True)
        place = jnp.where(mine > 0.0, rank.astype(I32) + turn * SPAN + 1, 0)
        pieces.append(jnp.sum(place, axis=0, keepdims=True) - 1)
    return jnp.concatenate(pieces, axis=1)


def to_slot_lanes(table, groups, n):
    rows = groups * SLOTS
    flat = n * SLOTS
    owner = hot((iota((n, flat), 1) >> 3) == iota((n, flat), 0))
    spread = picked(jnp.transpose(table)[:rows], owner, dot)
    keep = (iota((SLOTS, flat), 1) & 7) == iota((SLOTS, flat), 0)
    return [
        jnp.sum(jnp.where(keep, spread[g * SLOTS : (g + 1) * SLOTS], 0.0), axis=0, keepdims=True)
        for g in range(groups)
    ]


def pack_kernel(n, pos_ref, q_ref, g_ref, k_ref, v_ref, send_ref, slots_ref):
    tokens = q_ref.shape[0]
    width = q_ref.shape[1]
    quarters = pos_ref.shape[0] // ROUNDS
    before = hot(iota((tokens, tokens), 0) < iota((tokens, tokens), 1))
    rows = []
    for turn in range(ROUNDS):
        places = jnp.concatenate(
            [pos_ref[x * ROUNDS + turn : x * ROUNDS + turn + 1, :] for x in range(quarters)], axis=1
        )
        target = places >> 8
        member = iota((n, tokens), 0) == target
        earlier = dot(hot(member), before)
        rank = jnp.sum(jnp.where(member, earlier, 0.0), axis=0, keepdims=True).astype(I32)
        rows.append(target * SLOTS + turn * CAP + rank)
    slots_ref[...] = jnp.concatenate(rows + [jnp.zeros((8 - ROUNDS, tokens), I32)], axis=0)
    at = iota((n * SLOTS, tokens), 0)
    chosen = hot((at == rows[0]) | (at == rows[1]))
    filled = dot(chosen, jnp.ones((tokens, LANES), BF16))
    mark = jnp.where(iota((n * SLOTS, LANES), 1) == 0, EMPTY * (1.0 - filled), 0.0)
    first = dot(chosen, q_ref[...])
    send_ref[:, :LANES] = (first[:, :LANES] + mark).astype(BF16)
    send_ref[:, LANES:width] = first[:, LANES:].astype(BF16)
    for at_unit, ref in enumerate((g_ref, k_ref, v_ref)):
        send_ref[:, (at_unit + 1) * width : (at_unit + 2) * width] = dot(chosen, ref[...]).astype(BF16)


def unpack_kernel(n, recv_ref, qg_ref, kv_ref, code_ref):
    half = qg_ref.shape[1]
    flat = n * SLOTS
    lead = hot(iota((8, LANES), 1) == 0)
    first = dot_nt(lead, recv_ref[:, :LANES])
    code = compaction(first < EMPTY - 1.0, n)
    code_ref[...] = jnp.broadcast_to(code, code_ref.shape)
    chosen = hot(iota((ROUNDS * SPAN, flat), 0) == code)
    qg_ref[...] = dot(chosen, recv_ref[:, :half]).astype(BF16)
    kv_ref[...] = dot(chosen, recv_ref[:, half:]).astype(BF16)


def blocks(ref, turn, head, heads):
    rows = slice(turn * SPAN, (turn + 1) * SPAN)
    width = heads * HEAD_DIM
    lower = slice(head * HEAD_DIM, (head + 1) * HEAD_DIM)
    upper = slice(width + head * HEAD_DIM, width + (head + 1) * HEAD_DIM)
    return ref[rows, lower], ref[rows, upper]


def forward_kernel(n, qg_ref, kv_ref, front_ref, code_ref, table_ref, stats_ref):
    heads = qg_ref.shape[1] // (2 * HEAD_DIM)
    flat = n * SLOTS
    stats_ref[...] = jnp.zeros(stats_ref.shape, F32)
    for turn in range(ROUNDS):
        for head in range(heads):
            q, g = blocks(qg_ref, turn, head, heads)
            k, v = blocks(kv_ref, turn, head, heads)
            k_front, v_front = blocks(front_ref, turn, head, heads)
            score = dot_nt(k, q) * SCALE
            score_front = dot_nt(k_front, q) * SCALE
            highest = jnp.maximum(
                jnp.max(score, axis=0, keepdims=True), jnp.max(score_front, axis=0, keepdims=True)
            )
            raised = jnp.exp(score - highest)
            raised_front = jnp.exp(score_front - highest)
            total = jnp.sum(raised + raised_front, axis=0, keepdims=True)
            mixed = jnp.sum(
                raised * dot_nt(v, g) + raised_front * dot_nt(v_front, g), axis=0, keepdims=True
            )
            here = slice(turn * SPAN, (turn + 1) * SPAN)
            stats_ref[head : head + 1, here] = highest + jnp.log(total)
            stats_ref[heads + head : heads + head + 1, here] = mixed / total
    chosen = hot(iota((ROUNDS * SPAN, flat), 0) == code_ref[0:1, :])
    by_slot = picked(stats_ref[...], chosen, dot)
    keep = (iota((SLOTS, flat), 1) & 7) == iota((SLOTS, flat), 0)
    groups = [jnp.where(keep, by_slot[i : i + 1], 0.0) for i in range(2 * heads)]
    groups.append(jnp.zeros((LANES - 2 * heads * SLOTS, flat), F32))
    spread = jnp.concatenate(groups, axis=0)
    owner = hot((iota((n, flat), 1) >> 3) == iota((n, flat), 0))
    table_ref[...] = sum(dot_nt(owner, part.astype(BF16)) for part in three_parts(spread))


def home_kernel(n, heads, table_ref, slots_ref, back_ref):
    tokens = slots_ref.shape[1]
    rows = 2 * heads * SLOTS
    values = jnp.transpose(table_ref[...])[:rows]
    row_slot = iota((SLOTS, tokens), 0)
    members = []
    followers = []
    keeps = []
    logs = []
    dots = []
    for turn in range(ROUNDS):
        target, sub = slot_rows(slots_ref, turn)
        member = hot(iota((n, tokens), 0) == target)
        members.append(member)
        followers.append(hot(iota((n, tokens), 0) == ((target + n - 1) & (n - 1))))
        keep = row_slot == sub
        keeps.append(keep)
        here = picked(values, member, dot)
        read = [
            jnp.sum(jnp.where(keep, here[i * SLOTS : (i + 1) * SLOTS], 0.0), axis=0, keepdims=True)
            for i in range(2 * heads)
        ]
        logs.append(read[:heads])
        dots.append(read[heads:])
    shares = [[None] * heads for _ in range(ROUNDS)]
    means = []
    for head in range(heads):
        highest = jnp.maximum(logs[0][head], logs[1][head])
        raised = [jnp.exp(logs[turn][head] - highest) for turn in range(ROUNDS)]
        total = raised[0] + raised[1]
        for turn in range(ROUNDS):
            shares[turn][head] = raised[turn] / total
        means.append(shares[0][head] * dots[0][head] + shares[1][head] * dots[1][head])
    own = []
    behind = []
    one = jnp.ones((1, tokens), F32)
    for turn in range(ROUNDS):
        keep = keeps[turn]
        pieces = [jnp.where(keep, x, 0.0) for x in shares[turn] + means]
        more = [jnp.where(keep, x, 0.0) for x in logs[turn] + [one]]
        used = len(pieces) * SLOTS
        own.append(jnp.concatenate(pieces + [jnp.zeros((LANES - used, tokens), F32)], axis=0))
        both = len(pieces + more) * SLOTS
        behind.append(
            jnp.concatenate(
                [jnp.zeros((used, tokens), F32)]
                + pieces
                + more
                + [jnp.zeros((LANES - used - both, tokens), F32)],
                axis=0,
            )
        )
    result = jnp.zeros((n, LANES), F32)
    for onehot, spread in zip(members + followers, own + behind):
        for part in three_parts(spread):
            result = result + dot_nt(onehot, part.astype(BF16))
    back_ref[...] = result


def backward_kernel(
    n, qg_ref, kv_ref, front_ref, behind_ref, code_ref, stats_ref, back_ref, send_ref, grads_ref
):
    heads = qg_ref.shape[1] // (2 * HEAD_DIM)
    width = heads * HEAD_DIM
    flat = n * SLOTS
    count = 2 * heads
    rows = to_slot_lanes(back_ref[...], count + 3 * heads + 1, n)
    blank = jnp.zeros((8 - count, flat), F32)
    chosen = hot(iota((ROUNDS * SPAN, flat), 0) == code_ref[0:1, :])
    own = picked(jnp.concatenate(rows[:count] + [blank], axis=0), chosen, dot_nt)
    valid = jnp.broadcast_to(rows[-1], (8, flat)) > 0.5
    chosen_behind = hot(iota((ROUNDS * SPAN, flat), 0) == compaction(valid, n))
    blank = jnp.zeros((8 - 3 * heads, flat), F32)
    other = picked(jnp.concatenate(rows[count:-1] + [blank], axis=0), chosen_behind, dot_nt)
    for turn in range(ROUNDS):
        here = slice(turn * SPAN, (turn + 1) * SPAN)
        for head in range(heads):
            q, g = blocks(qg_ref, turn, head, heads)
            k, v = blocks(kv_ref, turn, head, heads)
            k_front, v_front = blocks(front_ref, turn, head, heads)
            q_behind, g_behind = blocks(behind_ref, turn, head, heads)

            def graded(keys, vals, queries, grads, log_total, share, mean):
                weighted = jnp.exp(dot_nt(keys, queries) * SCALE - log_total) * share
                grad_score = weighted * ((dot_nt(vals, grads) - mean) * SCALE)
                return weighted.astype(BF16), grad_score.astype(BF16)

            log_total = stats_ref[head : head + 1, here]
            share = own[head : head + 1, here]
            mean = own[heads + head : heads + head + 1, here]
            weight, scaled = graded(k, v, q, g, log_total, share, mean)
            _, scaled_front = graded(k_front, v_front, q, g, log_total, share, mean)
            weight_behind, scaled_behind = graded(
                k,
                v,
                q_behind,
                g_behind,
                other[2 * heads + head : 2 * heads + head + 1, here],
                other[head : head + 1, here],
                other[heads + head : heads + head + 1, here],
            )
            grad_q = dot_tn(scaled, k) + dot_tn(scaled_front, k_front)
            grad_k = dot(scaled, q) + dot(scaled_behind, q_behind)
            grad_v = dot(weight, g) + dot(weight_behind, g_behind)
            for unit, grad in enumerate((grad_q, grad_k, grad_v)):
                at = unit * width + head * HEAD_DIM
                grads_ref[here, at : at + HEAD_DIM] = grad.astype(BF16)
    send_ref[...] = dot_tn(chosen, grads_ref[...]).astype(BF16)


def final_kernel(slots_ref, ret_ref, dq_ref, dk_ref, dv_ref):
    tokens = slots_ref.shape[1]
    width = dq_ref.shape[1]
    at = iota((ret_ref.shape[0], tokens), 0)
    chosen = hot((at == slots_ref[0:1, :]) | (at == slots_ref[1:2, :]))
    for unit, ref in enumerate((dq_ref, dk_ref, dv_ref)):
        ref[...] = dot_tn(chosen, ret_ref[:, unit * width : (unit + 1) * width]).astype(BF16)


def call(kernel, out, name, scratch=()):
    return pl.pallas_call(
        kernel,
        out_shape=out,
        scratch_shapes=scratch,
        name=name,
        compiler_params=pltpu.CompilerParams(vmem_limit_bytes=48 * 1024 * 1024),
    )


def shape(*dims, dtype=BF16):
    return jax.ShapeDtypeStruct(dims, dtype)


def exchanged(block):
    return lax.all_to_all(block, "seq", split_axis=0, concat_axis=0, tiled=True)


def passed_along(block, distance):
    n = lax.axis_size("seq")
    return lax.ppermute(block, "seq", [((i - distance) % n, i) for i in range(n)])


def body(queries, keys, values, out_grad, sorted_position):
    n = lax.axis_size("seq")
    tokens, width = queries.shape
    heads = width // HEAD_DIM
    flat = n * SLOTS
    places = ROUNDS * SPAN
    placed = lax.all_gather(sorted_position, "head", axis=0, tiled=True)
    send, slots = call(
        functools.partial(pack_kernel, n),
        (shape(flat, 4 * width), shape(8, tokens, dtype=I32)),
        "pack",
    )(placed, queries, out_grad, keys, values)
    arrived = exchanged(send)
    qg, kv, code = call(
        functools.partial(unpack_kernel, n),
        (shape(places, 2 * width), shape(places, 2 * width), shape(8, flat, dtype=I32)),
        "unpack",
    )(arrived)
    front = passed_along(kv, 1)
    behind = passed_along(qg, -1)
    table, stats = call(
        functools.partial(forward_kernel, n),
        (shape(n, LANES, dtype=F32), shape(8, places, dtype=F32)),
        "forward",
    )(qg, kv, front, code)
    back = call(functools.partial(home_kernel, n, heads), shape(n, LANES, dtype=F32), "home")(
        exchanged(table), slots
    )
    grads = call(
        functools.partial(backward_kernel, n),
        shape(flat, 3 * width),
        "backward",
        [pltpu.VMEM((places, 3 * width), BF16)],
    )(qg, kv, front, behind, code, stats, exchanged(back))
    return call(final_kernel, (shape(tokens, width),) * 3, "final")(slots, exchanged(grads))


def solution(mesh):
    in_specs = (
        P("seq", "head"),
        P("seq", "head"),
        P("seq", "head"),
        P("seq", "head"),
        P(None, ("seq", "head")),
    )
    out_specs = (P("seq", "head"), P("seq", "head"), P("seq", "head"))
    return jax.shard_map(body, mesh=mesh, in_specs=in_specs, out_specs=out_specs, check_vma=False)
```

```python
import functools
import math

import jax
import jax.numpy as jnp
from jax import lax
from jax.experimental import pallas as pl
from jax.experimental.pallas import tpu as pltpu
from jax.sharding import PartitionSpec as P

HEAD_DIM = 128
SPAN = 256
ROUNDS = 2
CAP = 4
GROUP = 4
SLOTS = 8
HALVES = 2
LANES = 128
EMPTY = 8.0
SCALE = 1.0 / math.sqrt(HEAD_DIM)
F32 = jnp.float32
BF16 = jnp.bfloat16
I32 = jnp.int32


def iota(shape, dim):
    return lax.broadcasted_iota(I32, shape, dim)


def hot(condition):
    return jnp.where(condition, 1.0, 0.0).astype(BF16)


def dot(a, b):
    return lax.dot_general(a, b, (((1,), (0,)), ((), ())), preferred_element_type=F32)


def dot_nt(a, b):
    return lax.dot_general(a, b, (((1,), (1,)), ((), ())), preferred_element_type=F32)


def dot_tn(a, b):
    return lax.dot_general(a, b, (((0,), (0,)), ((), ())), preferred_element_type=F32)


def three_parts(x):
    high = x.astype(BF16).astype(F32)
    rest = x - high
    middle = rest.astype(BF16).astype(F32)
    return high, middle, (rest - middle).astype(BF16).astype(F32)


def picked(x, onehot, product):
    rows = x.shape[0]
    stacked = jnp.concatenate(three_parts(x), axis=0).astype(BF16)
    out = product(stacked, onehot)
    return out[:rows] + out[rows : 2 * rows] + out[2 * rows :]


def hot_rows(code):
    at = iota((SPAN, LANES), 0).astype(F32).astype(BF16)
    code = code.astype(F32).astype(BF16)
    pieces = [
        jnp.where(at == code[:, i : i + LANES], jnp.ones_like(at), jnp.zeros_like(at))
        for i in range(0, code.shape[1], LANES)
    ]
    return jnp.concatenate(pieces, axis=1)


def ranked(mine):
    before = hot(iota((LANES, LANES), 0) < iota((LANES, LANES), 1))
    chunks = mine.shape[1] // LANES
    stacked = jnp.concatenate([mine[:, i * LANES : (i + 1) * LANES] for i in range(chunks)], axis=0)
    rank = dot(stacked.astype(BF16), before)
    totals = jnp.sum(stacked, axis=1, keepdims=True)
    running = jnp.zeros((8, 1), F32)
    pieces = []
    for i in range(chunks):
        here = slice(i * 8, (i + 1) * 8)
        pieces.append(jnp.where(stacked[here] > 0.0, rank[here] + running, -1.0))
        running = running + totals[here]
    return jnp.concatenate(pieces, axis=1).astype(I32)


def to_slot_lanes(table, groups, n):
    rows = groups * SLOTS
    flat = n * SLOTS
    owner = hot((iota((n, flat), 1) >> 3) == iota((n, flat), 0))
    spread = picked(jnp.transpose(table)[:rows], owner, dot)
    keep = (iota((SLOTS, flat), 1) & 7) == iota((SLOTS, flat), 0)
    return [
        jnp.sum(jnp.where(keep, spread[g * SLOTS : (g + 1) * SLOTS], 0.0), axis=0, keepdims=True)
        for g in range(groups)
    ]


def pack_kernel(n, pos_ref, held_ref, send_ref, slots_ref):
    tokens = held_ref.shape[0]
    width = held_ref.shape[1] // 4
    quarters = pos_ref.shape[0] // ROUNDS
    groups = n // GROUP
    tall = groups * SLOTS
    before = hot(iota((tokens, tokens), 0) < iota((tokens, tokens), 1))
    main = [[], []]
    edge = []
    slots = []
    for turn in range(ROUNDS):
        places = jnp.concatenate(
            [pos_ref[x * ROUNDS + turn : x * ROUNDS + turn + 1, :] for x in range(quarters)], axis=1
        )
        span = places >> 8
        member = iota((n, tokens), 0) == span
        earlier = dot(hot(member), before)
        rank = jnp.sum(jnp.where(member, earlier, 0.0), axis=0, keepdims=True).astype(I32)
        slots.append(span * CAP + rank)
        row = (span >> 2) * SLOTS + (span & 1) * CAP + rank
        for half in range(HALVES):
            main[half].append(hot_rows(jnp.where(((span >> 1) & 1) == half, row, -1)))
        last = (span & 3) == 3
        row = (((span + 1) & (n - 1)) >> 2) * SLOTS + rank
        edge.append(
            hot_rows(jnp.where(last, row, -1)) + hot_rows(jnp.where(last, row + CAP, -1))
        )
    slots_ref[...] = jnp.concatenate(slots + [jnp.zeros((8 - ROUNDS, tokens), I32)], axis=0)
    chosen = jnp.concatenate(main[0] + main[1] + edge, axis=0)
    filled = dot(chosen, jnp.ones((tokens, LANES), BF16))
    mark = jnp.where(iota(filled.shape, 1) == 0, EMPTY * (1.0 - filled), 0.0)
    mark = jnp.concatenate([mark] * (width // LANES), axis=1)

    def store(column, part):
        tiles = [
            part[turn * tall : (turn + 1) * tall, head * HEAD_DIM : (head + 1) * HEAD_DIM].reshape(
                groups, 1, SLOTS, HEAD_DIM
            )
            for turn in range(ROUNDS)
            for head in range(part.shape[1] // HEAD_DIM)
        ]
        rows = jnp.concatenate(tiles, axis=1).reshape(n * SLOTS, HEAD_DIM)
        send_ref[:, column * HEAD_DIM : (column + 1) * HEAD_DIM] = rows.astype(BF16)

    both = ROUNDS * tall
    edges = []
    for unit in range(4):
        rows = chosen if unit >= 2 else chosen[: HALVES * both]
        part = dot(rows, held_ref[:, unit * width : (unit + 1) * width])
        for half in range(HALVES):
            rows = slice(half * both, (half + 1) * both)
            store(half * 4 + unit, part[rows] + mark[rows] if unit == 0 else part[rows])
        edges.append(part[HALVES * both :])
    upper = (iota(edges[2].shape, 0) & CAP) == 0
    store(HALVES * 4, jnp.where(upper, edges[2], edges[3]) + mark[HALVES * both :])


def unpack_kernel(n, recv_ref, rows_ref, front_ref, head_ref, code_ref, chosen_ref):
    flat = n * SLOTS
    wide = 4 * HEAD_DIM
    lead = hot(iota((8, LANES), 1) == 0)
    row = iota((8, flat), 0)
    mine = jnp.zeros((8, flat), F32)
    for block in range(HALVES + 1):
        first = dot_nt(lead, recv_ref[:, block * wide : block * wide + LANES])
        mine = jnp.where(((row >> 1) == block) & (first < EMPTY - 1.0), 1.0, mine)
    mine = jnp.where(((iota((8, flat), 1) >> 2) & 1) == (row & 1), mine, 0.0)
    code = ranked(mine)
    code_ref[...] = code
    for half in range(HALVES):
        here = slice(half * 2 * SPAN, (half + 1) * 2 * SPAN)
        chosen = jnp.concatenate(
            [hot_rows(code[half * 2 + span : half * 2 + span + 1]) for span in range(2)], axis=0
        )
        chosen_ref[here, :] = chosen
        rows = dot(chosen, recv_ref[:, half * wide : (half + 1) * wide]).astype(BF16)
        rows_ref[here, :] = rows
        if half == 0:
            head_ref[...] = rows[:SPAN, : 2 * HEAD_DIM]
    for kind in range(2):
        chosen = hot_rows(code[2 * HALVES + kind : 2 * HALVES + kind + 1])
        front_ref[kind * SPAN : (kind + 1) * SPAN, :] = dot(
            chosen, recv_ref[:, HALVES * wide : HALVES * wide + LANES]
        ).astype(BF16)


def unit_of(ref, span, unit):
    return ref[span * SPAN : (span + 1) * SPAN, unit * HEAD_DIM : (unit + 1) * HEAD_DIM]


def forward_kernel(n, rows_ref, front_ref, chosen_ref, table_ref, stats_ref):
    flat = n * SLOTS
    stats_ref[...] = jnp.zeros(stats_ref.shape, F32)
    for span in range(GROUP):
        q, g, k, v = (unit_of(rows_ref, span, unit) for unit in range(4))
        if span == 0:
            k_front, v_front = unit_of(front_ref, 0, 0), unit_of(front_ref, 1, 0)
        else:
            k_front, v_front = unit_of(rows_ref, span - 1, 2), unit_of(rows_ref, span - 1, 3)
        score = dot_nt(k, q) * SCALE
        score_front = dot_nt(k_front, q) * SCALE
        highest = jnp.maximum(
            jnp.max(score, axis=0, keepdims=True), jnp.max(score_front, axis=0, keepdims=True)
        )
        raised = jnp.exp(score - highest)
        raised_front = jnp.exp(score_front - highest)
        total = jnp.sum(raised + raised_front, axis=0, keepdims=True)
        mixed = jnp.sum(
            raised * dot_nt(v, g) + raised_front * dot_nt(v_front, g), axis=0, keepdims=True
        )
        here = slice(span * SPAN, (span + 1) * SPAN)
        stats_ref[0:1, here] = highest + jnp.log(total)
        stats_ref[1:2, here] = mixed / total
    keep = (iota((SLOTS, flat), 1) & 7) == iota((SLOTS, flat), 0)
    by_half = []
    for half in range(HALVES):
        here = slice(half * 2 * SPAN, (half + 1) * 2 * SPAN)
        by_half.append(picked(stats_ref[:, here], chosen_ref[here, :], dot))
    spread = [
        jnp.where(keep, by_half[half][kind : kind + 1], 0.0)
        for kind in range(2)
        for half in range(HALVES)
    ]
    spread.append(jnp.zeros((LANES - len(spread) * SLOTS, flat), F32))
    spread = jnp.concatenate(spread, axis=0)
    owner = hot((iota((n, flat), 1) >> 3) == iota((n, flat), 0))
    table_ref[...] = sum(dot_nt(owner, part.astype(BF16)) for part in three_parts(spread))


def home_kernel(n, heads, table_ref, slots_ref, back_ref):
    tokens = slots_ref.shape[1]
    wide = GROUP * CAP
    values = jnp.transpose(table_ref[...])[: 2 * wide]
    device = iota((n, tokens), 0)
    lane = iota((wide, tokens), 0)
    span_slot = []
    logs = []
    dots = []
    for turn in range(ROUNDS):
        slot = slots_ref[turn : turn + 1, :]
        group = slot >> 4
        keep = lane == (slot & 15)
        span_slot.append((group, keep, slot))
        for head in range(heads):
            member = hot(device == group * GROUP + turn * heads + head)
            here = picked(values, member, dot)
            logs.append(jnp.sum(jnp.where(keep, here[:wide], 0.0), axis=0, keepdims=True))
            dots.append(jnp.sum(jnp.where(keep, here[wide:], 0.0), axis=0, keepdims=True))
    members = []
    values = []
    one = jnp.ones((1, tokens), F32)
    for head in range(heads):
        log_0, log_1 = logs[head], logs[heads + head]
        highest = jnp.maximum(log_0, log_1)
        raised = [jnp.exp(log_0 - highest), jnp.exp(log_1 - highest)]
        total = raised[0] + raised[1]
        shares = [raised[0] / total, raised[1] / total]
        mean = shares[0] * dots[head] + shares[1] * dots[heads + head]
        for turn in range(ROUNDS):
            group, keep, slot = span_slot[turn]
            mine = turn * heads + head
            members.append(hot(device == group * GROUP + mine))
            values.append(
                jnp.concatenate(
                    [jnp.where(keep, x, 0.0) for x in (shares[turn], mean)]
                    + [jnp.zeros((LANES - 2 * wide, tokens), F32)],
                    axis=0,
                )
            )
            ahead = ((group + n // GROUP - 1) & (n // GROUP - 1)) * GROUP + mine
            members.append(hot(device == ahead))
            edge = iota((SLOTS, tokens), 0) == jnp.where((slot & 12) == 0, slot & 3, -1)
            values.append(
                jnp.concatenate(
                    [jnp.zeros((2 * wide, tokens), F32)]
                    + [jnp.where(edge, x, 0.0) for x in (shares[turn], mean, logs[mine], one)]
                    + [jnp.zeros((LANES - 2 * wide - 4 * SLOTS, tokens), F32)],
                    axis=0,
                )
            )
    left = jnp.concatenate(members, axis=1)
    right = jnp.concatenate(values, axis=1)
    back_ref[...] = sum(dot_nt(left, part.astype(BF16)) for part in three_parts(right))


def backward_kernel(
    n,
    rows_ref,
    front_ref,
    behind_ref,
    chosen_ref,
    code_ref,
    stats_ref,
    back_ref,
    send_ref,
    grads_ref,
):
    flat = n * SLOTS
    lanes = to_slot_lanes(back_ref[...], 2 * HALVES + 4, n)
    shares = []
    means = []
    for half in range(HALVES):
        chosen = chosen_ref[half * 2 * SPAN : (half + 1) * 2 * SPAN, :]
        pair = jnp.concatenate(
            [lanes[half], lanes[HALVES + half], jnp.zeros((6, flat), F32)], axis=0
        )
        own = picked(pair, chosen, dot_nt)
        for span in range(2):
            shares.append(own[0:1, span * SPAN : (span + 1) * SPAN])
            means.append(own[1:2, span * SPAN : (span + 1) * SPAN])
    edge = lanes[2 * HALVES :]
    chosen = hot_rows(ranked(jnp.broadcast_to(edge[3], (8, flat)))[0:1])
    other = picked(
        jnp.concatenate(edge[:3] + [jnp.zeros((5, flat), F32)], axis=0), chosen, dot_nt
    )

    def graded(keys, vals, queries, grads, log_total, share, mean):
        weighted = jnp.exp(dot_nt(keys, queries) * SCALE - log_total) * share
        grad_score = weighted * ((dot_nt(vals, grads) - mean) * SCALE)
        return weighted.astype(BF16), grad_score.astype(BF16)

    def put(span, unit, grad):
        grads_ref[span * SPAN : (span + 1) * SPAN, unit * HEAD_DIM : (unit + 1) * HEAD_DIM] = (
            grad.astype(BF16)
        )

    grad_k = None
    grad_v = None
    for span in range(GROUP):
        q, g, k, v = (unit_of(rows_ref, span, unit) for unit in range(4))
        log_total = stats_ref[0:1, span * SPAN : (span + 1) * SPAN]
        if span == 0:
            k_front, v_front = unit_of(front_ref, 0, 0), unit_of(front_ref, 1, 0)
        else:
            k_front, v_front = unit_of(rows_ref, span - 1, 2), unit_of(rows_ref, span - 1, 3)
        row = (log_total, shares[span], means[span])
        weight, scaled = graded(k, v, q, g, *row)
        weight_front, scaled_front = graded(k_front, v_front, q, g, *row)
        put(span, 0, dot_tn(scaled, k) + dot_tn(scaled_front, k_front))
        if span > 0:
            put(span - 1, 1, grad_k + dot(scaled_front, q))
            put(span - 1, 2, grad_v + dot(weight_front, g))
        grad_k = dot(scaled, q)
        grad_v = dot(weight, g)
    q, g = behind_ref[:, :HEAD_DIM], behind_ref[:, HEAD_DIM:]
    weight, scaled = graded(k, v, q, g, other[2:3], other[0:1], other[1:2])
    put(GROUP - 1, 1, grad_k + dot(scaled, q))
    put(GROUP - 1, 2, grad_v + dot(weight, g))
    wide = 3 * HEAD_DIM
    codes = jnp.transpose(code_ref[...].astype(F32)).astype(I32)
    for half in range(HALVES):
        across = jnp.concatenate(
            [hot(iota((flat, SPAN), 1) == codes[:, i : i + 1]) for i in (half * 2, half * 2 + 1)],
            axis=1,
        )
        send_ref[:, half * wide : (half + 1) * wide] = dot(
            across, grads_ref[half * 2 * SPAN : (half + 1) * 2 * SPAN, :]
        ).astype(BF16)


def final_kernel(n, slots_ref, ret_ref, dq_ref, dk_ref, dv_ref):
    heads = dq_ref.shape[1] // HEAD_DIM
    flat = n * SLOTS
    wide = 3 * HEAD_DIM
    slots = jnp.transpose(slots_ref[...].astype(F32)).astype(I32)
    at = iota((slots.shape[0], flat), 1)
    for head in range(heads):
        total = None
        for half in range(HALVES):
            match = []
            for turn in range(ROUNDS):
                slot = slots[:, turn : turn + 1]
                row = ((slot >> 4) * GROUP + turn * heads + head) * SLOTS + (slot & 7)
                match.append(at == jnp.where(((slot >> 3) & 1) == half, row, -1))
            part = dot(hot(match[0] | match[1]), ret_ref[:, half * wide : (half + 1) * wide])
            total = part if total is None else total + part
        for unit, ref in enumerate((dq_ref, dk_ref, dv_ref)):
            ref[:, head * HEAD_DIM : (head + 1) * HEAD_DIM] = total[
                :, unit * HEAD_DIM : (unit + 1) * HEAD_DIM
            ].astype(BF16)


def call(kernel, out, name, scratch=()):
    return pl.pallas_call(
        kernel,
        out_shape=out,
        scratch_shapes=scratch,
        name=name,
        compiler_params=pltpu.CompilerParams(vmem_limit_bytes=24 * 1024 * 1024),
    )


def shape(*dims, dtype=BF16):
    return jax.ShapeDtypeStruct(dims, dtype)


def exchanged(block):
    return lax.all_to_all(block, "seq", split_axis=0, concat_axis=0, tiled=True)


def passed_along(block, distance):
    n = lax.axis_size("seq")
    return lax.ppermute(block, "seq", [((i - distance) % n, i) for i in range(n)])


def body(queries, keys, values, out_grad, sorted_position):
    n = lax.axis_size("seq")
    tokens, width = queries.shape
    heads = width // HEAD_DIM
    flat = n * SLOTS
    places = GROUP * SPAN
    placed = lax.all_gather(sorted_position, "head", axis=0, tiled=True)
    send, slots = call(
        functools.partial(pack_kernel, n),
        (shape(flat, (4 * HALVES + 1) * HEAD_DIM), shape(8, tokens, dtype=I32)),
        "pack",
    )(placed, jnp.concatenate([queries, out_grad, keys, values], axis=1))
    rows, front, first, code, chosen = call(
        functools.partial(unpack_kernel, n),
        (
            shape(places, 4 * HEAD_DIM),
            shape(2 * SPAN, HEAD_DIM),
            shape(SPAN, 2 * HEAD_DIM),
            shape(8, flat, dtype=I32),
            shape(places, flat),
        ),
        "unpack",
    )(exchanged(send))
    behind = passed_along(first, -GROUP)
    table, stats = call(
        functools.partial(forward_kernel, n),
        (shape(n, LANES, dtype=F32), shape(8, places, dtype=F32)),
        "forward",
    )(rows, front, chosen)
    back = call(functools.partial(home_kernel, n, heads), shape(n, LANES, dtype=F32), "home")(
        exchanged(table), slots
    )
    grads = call(
        functools.partial(backward_kernel, n),
        shape(flat, 3 * HALVES * HEAD_DIM),
        "backward",
        [pltpu.VMEM((places, 3 * HEAD_DIM), BF16)],
    )(rows, front, behind, chosen, code, stats, exchanged(back))
    return call(functools.partial(final_kernel, n), (shape(tokens, width),) * 3, "final")(
        slots, exchanged(grads)
    )


def solution(mesh):
    in_specs = (
        P("seq", "head"),
        P("seq", "head"),
        P("seq", "head"),
        P("seq", "head"),
        P(None, ("seq", "head")),
    )
    out_specs = (P("seq", "head"), P("seq", "head"), P("seq", "head"))
    return jax.shard_map(body, mesh=mesh, in_specs=in_specs, out_specs=out_specs, check_vma=False)
```

```python
import functools
import math

import jax
import jax.numpy as jnp
from jax import lax
from jax.experimental import pallas as pl
from jax.experimental.pallas import tpu as pltpu
from jax.sharding import PartitionSpec as P

HEAD_DIM = 128
SPAN = 256
ROUNDS = 2
CAP = 4
GROUP = 4
SLOTS = 8
HALVES = 2
LANES = 128
EMPTY = 8.0
SCALE = 1.0 / math.sqrt(HEAD_DIM)
F32 = jnp.float32
BF16 = jnp.bfloat16
I32 = jnp.int32


def iota(shape, dim):
    return lax.broadcasted_iota(I32, shape, dim)


def hot(condition):
    return jnp.where(condition, 1.0, 0.0).astype(BF16)


def dot(a, b):
    return lax.dot_general(a, b, (((1,), (0,)), ((), ())), preferred_element_type=F32)


def dot_nt(a, b):
    return lax.dot_general(a, b, (((1,), (1,)), ((), ())), preferred_element_type=F32)


def dot_tn(a, b):
    return lax.dot_general(a, b, (((0,), (0,)), ((), ())), preferred_element_type=F32)


def three_parts(x):
    high = x.astype(BF16).astype(F32)
    rest = x - high
    middle = rest.astype(BF16).astype(F32)
    return high, middle, (rest - middle).astype(BF16).astype(F32)


def picked(x, onehot, product):
    rows = x.shape[0]
    stacked = jnp.concatenate(three_parts(x), axis=0).astype(BF16)
    out = product(stacked, onehot)
    return out[:rows] + out[rows : 2 * rows] + out[2 * rows :]


def hot_rows(code, rows=SPAN):
    at = iota((rows, LANES), 0).astype(F32).astype(BF16)
    code = code.astype(F32).astype(BF16)
    pieces = [
        jnp.where(at == code[:, i : i + LANES], jnp.ones_like(at), jnp.zeros_like(at))
        for i in range(0, code.shape[1], LANES)
    ]
    return jnp.concatenate(pieces, axis=1)


def ranked(mine):
    before = hot(iota((LANES, LANES), 0) < iota((LANES, LANES), 1))
    chunks = mine.shape[1] // LANES
    stacked = jnp.concatenate([mine[:, i * LANES : (i + 1) * LANES] for i in range(chunks)], axis=0)
    rank = dot(stacked.astype(BF16), before)
    totals = jnp.sum(stacked, axis=1, keepdims=True)
    running = jnp.zeros((8, 1), F32)
    pieces = []
    for i in range(chunks):
        here = slice(i * 8, (i + 1) * 8)
        pieces.append(jnp.where(stacked[here] > 0.0, rank[here] + running, -1.0))
        running = running + totals[here]
    return jnp.concatenate(pieces, axis=1).astype(I32)


def pack_kernel(n, pos_ref, held_ref, send_ref, slots_ref):
    tokens = held_ref.shape[0]
    width = held_ref.shape[1] // 4
    heads = width // HEAD_DIM
    quarters = pos_ref.shape[0] // ROUNDS
    tall = n // GROUP * SLOTS
    before = hot(iota((tokens, tokens), 0) < iota((tokens, tokens), 1))
    main = [[], []]
    edge = []
    slots = []
    for turn in range(ROUNDS):
        places = jnp.concatenate(
            [pos_ref[x * ROUNDS + turn : x * ROUNDS + turn + 1, :] for x in range(quarters)], axis=1
        )
        span = places >> 8
        member = hot_rows(span, n)
        earlier = dot(member, before)
        rank = jnp.sum(member.astype(F32) * earlier, axis=0, keepdims=True).astype(I32)
        slots.append(span * CAP + rank)
        row = (span >> 2) * SLOTS + (span & 1) * CAP + rank
        for half in range(HALVES):
            main[half].append(hot_rows(jnp.where(((span >> 1) & 1) == half, row, -1)))
        last = (span & 3) == 3
        row = (((span + 1) & (n - 1)) >> 2) * SLOTS + rank
        edge.append(
            hot_rows(jnp.where(last, row, -1)) + hot_rows(jnp.where(last, row + CAP, -1))
        )
    slots_ref[...] = jnp.concatenate(slots + [jnp.zeros((8 - ROUNDS, tokens), I32)], axis=0)
    chosen = jnp.concatenate(main[0] + main[1] + edge, axis=0)
    filled = dot(chosen, jnp.ones((tokens, LANES), BF16))
    mark = jnp.where(iota(filled.shape, 1) == 0, EMPTY * (1.0 - filled), 0.0)

    def store(column, part):
        for head in range(heads):
            rows = slice(head * ROUNDS * tall, (head + 1) * ROUNDS * tall)
            send_ref[rows, column * HEAD_DIM : (column + 1) * HEAD_DIM] = part[
                :, head * HEAD_DIM : (head + 1) * HEAD_DIM
            ].astype(BF16)

    both = ROUNDS * tall
    edges = []
    for unit in range(4):
        rows = chosen if unit >= 2 else chosen[: HALVES * both]
        part = dot(rows, held_ref[:, unit * width : (unit + 1) * width])
        if unit == 0:
            part = part + jnp.concatenate([mark[: HALVES * both]] * heads, axis=1)
        for half in range(HALVES):
            store(half * 4 + unit, part[half * both : (half + 1) * both])
        edges.append(part[HALVES * both :])
    upper = (iota(edges[2].shape, 0) & CAP) == 0
    mark = jnp.concatenate([mark[HALVES * both :]] * heads, axis=1)
    store(HALVES * 4, jnp.where(upper, edges[2], edges[3]) + mark)


def unpack_kernel(n, recv_ref, rows_ref, front_ref, head_ref, info_ref):
    flat = n * SLOTS
    wide = 4 * HEAD_DIM
    lead = hot(iota((8, LANES), 1) == 0)
    row = iota((8, flat), 0)
    mine = jnp.zeros((8, flat), F32)
    for block in range(HALVES + 1):
        first = dot_nt(lead, recv_ref[:, block * wide : block * wide + LANES])
        mine = jnp.where(((row >> 1) == block) & (first < EMPTY - 1.0), 1.0, mine)
    mine = jnp.where(((iota((8, flat), 1) >> 2) & 1) == (row & 1), mine, 0.0)
    code = ranked(mine)
    at = iota((flat, LANES), 0)
    lane = iota((flat, LANES), 1)
    origin = jnp.where(lane == 0, at >> 3, jnp.where(lane == 1, at & 7, 0))
    origin = origin.astype(F32).astype(BF16)
    for half in range(HALVES):
        here = slice(half * 2 * SPAN, (half + 1) * 2 * SPAN)
        chosen = jnp.concatenate(
            [hot_rows(code[half * 2 + span : half * 2 + span + 1]) for span in range(2)], axis=0
        )
        rows = dot(chosen, recv_ref[:, half * wide : (half + 1) * wide]).astype(BF16)
        rows_ref[here, :] = rows
        info = jnp.transpose(dot(chosen, origin))[:8]
        info_ref[:, here] = info
        if half == 0:
            head_ref[:SPAN, :] = rows[:SPAN, : 2 * HEAD_DIM]
            head_ref[SPAN:, :] = jnp.concatenate(
                [info[:, :SPAN], jnp.zeros((8, SPAN), F32)], axis=0
            ).astype(BF16)
    for kind in range(2):
        chosen = hot_rows(code[2 * HALVES + kind : 2 * HALVES + kind + 1])
        front_ref[kind * SPAN : (kind + 1) * SPAN, :] = dot(
            chosen, recv_ref[:, HALVES * wide : HALVES * wide + LANES]
        ).astype(BF16)


def unit_of(ref, span, unit):
    return ref[span * SPAN : (span + 1) * SPAN, unit * HEAD_DIM : (unit + 1) * HEAD_DIM]


def forward_kernel(n, rows_ref, front_ref, info_ref, table_ref, stats_ref):
    stats_ref[...] = jnp.zeros(stats_ref.shape, F32)
    for span in range(GROUP):
        q, g, k, v = (unit_of(rows_ref, span, unit) for unit in range(4))
        if span == 0:
            k_front, v_front = unit_of(front_ref, 0, 0), unit_of(front_ref, 1, 0)
        else:
            k_front, v_front = unit_of(rows_ref, span - 1, 2), unit_of(rows_ref, span - 1, 3)
        score = dot_nt(k, q) * SCALE
        score_front = dot_nt(k_front, q) * SCALE
        highest = jnp.maximum(
            jnp.max(score, axis=0, keepdims=True), jnp.max(score_front, axis=0, keepdims=True)
        )
        raised = jnp.exp(score - highest)
        raised_front = jnp.exp(score_front - highest)
        total = jnp.sum(raised + raised_front, axis=0, keepdims=True)
        mixed = jnp.sum(
            raised * dot_nt(v, g) + raised_front * dot_nt(v_front, g), axis=0, keepdims=True
        )
        here = slice(span * SPAN, (span + 1) * SPAN)
        stats_ref[0:1, here] = highest + jnp.log(total)
        stats_ref[1:2, here] = mixed / total
    places = stats_ref.shape[1]
    slot = iota((SLOTS, places), 0) == info_ref[1:2, :].astype(I32)
    upper = iota((SLOTS, places), 1) >= 2 * SPAN
    spread = [
        jnp.where(slot & (upper == (half == 1)), stats_ref[kind : kind + 1, :], 0.0)
        for kind in range(2)
        for half in range(HALVES)
    ]
    spread.append(jnp.zeros((LANES - len(spread) * SLOTS, places), F32))
    spread = jnp.concatenate(spread, axis=0)
    owner = hot_rows(info_ref[0:1, :], n)
    table_ref[...] = sum(dot_nt(owner, part.astype(BF16)) for part in three_parts(spread))


def home_kernel(n, heads, table_ref, slots_ref, back_ref):
    tokens = slots_ref.shape[1]
    wide = GROUP * CAP
    groups = n // GROUP
    values = jnp.transpose(table_ref[...])[: 2 * wide]
    lane = iota((wide, tokens), 0)
    span_slot = []
    logs = []
    dots = []
    for turn in range(ROUNDS):
        slot = slots_ref[turn : turn + 1, :]
        group = slot >> 4
        keep = lane == (slot & 15)
        span_slot.append((group, keep, slot))
        for head in range(heads):
            member = hot_rows((head * ROUNDS + turn) * groups + group, n)
            here = picked(values, member, dot)
            logs.append(jnp.sum(jnp.where(keep, here[:wide], 0.0), axis=0, keepdims=True))
            dots.append(jnp.sum(jnp.where(keep, here[wide:], 0.0), axis=0, keepdims=True))
    members = []
    values = []
    for head in range(heads):
        log_0, log_1 = logs[head], logs[heads + head]
        highest = jnp.maximum(log_0, log_1)
        raised = [jnp.exp(log_0 - highest), jnp.exp(log_1 - highest)]
        total = raised[0] + raised[1]
        shares = [raised[0] / total, raised[1] / total]
        mean = shares[0] * dots[head] + shares[1] * dots[heads + head]
        for turn in range(ROUNDS):
            group, keep, slot = span_slot[turn]
            first = (head * ROUNDS + turn) * groups
            members.append(hot_rows(first + group, n))
            values.append(
                jnp.concatenate(
                    [jnp.where(keep, x, 0.0) for x in (shares[turn], mean)]
                    + [jnp.zeros((LANES - 2 * wide, tokens), F32)],
                    axis=0,
                )
            )
            members.append(hot_rows(first + ((group + groups - 1) & (groups - 1)), n))
            edge = iota((SLOTS, tokens), 0) == jnp.where((slot & 12) == 0, slot & 3, -1)
            values.append(
                jnp.concatenate(
                    [jnp.zeros((2 * wide, tokens), F32)]
                    + [jnp.where(edge, x, 0.0) for x in (shares[turn], mean, logs[turn * heads + head])]
                    + [jnp.zeros((LANES - 2 * wide - 3 * SLOTS, tokens), F32)],
                    axis=0,
                )
            )
    left = jnp.concatenate(members, axis=1)
    right = jnp.concatenate(values, axis=1)
    back_ref[...] = sum(dot_nt(left, part.astype(BF16)) for part in three_parts(right))


def backward_kernel(
    n, rows_ref, front_ref, behind_ref, info_ref, stats_ref, back_ref, send_ref, grads_ref
):
    flat = n * SLOTS
    places = info_ref.shape[1]
    values = jnp.transpose(back_ref[...])
    source = info_ref[0:1, :].astype(I32)
    slot = info_ref[1:2, :].astype(I32)
    keep = iota((SLOTS, places), 0) == slot
    upper = iota((SLOTS, places), 1) >= 2 * SPAN
    here = picked(values[: 4 * SLOTS], hot_rows(source, n), dot)
    own = []
    for kind in range(2):
        low = here[2 * kind * SLOTS : (2 * kind + 1) * SLOTS]
        high = here[(2 * kind + 1) * SLOTS : (2 * kind + 2) * SLOTS]
        own.append(
            jnp.sum(jnp.where(keep, jnp.where(upper, high, low), 0.0), axis=0, keepdims=True)
        )
    info = behind_ref[SPAN:, :].astype(F32).astype(I32)
    here = picked(values[4 * SLOTS : 7 * SLOTS], hot_rows(info[0:1], n), dot)
    keep = iota((SLOTS, SPAN), 0) == info[1:2]
    other = [
        jnp.sum(jnp.where(keep, here[i * SLOTS : (i + 1) * SLOTS], 0.0), axis=0, keepdims=True)
        for i in range(3)
    ]

    def graded(keys, vals, queries, grads, log_total, share, mean):
        weighted = jnp.exp(dot_nt(keys, queries) * SCALE - log_total) * share
        grad_score = weighted * ((dot_nt(vals, grads) - mean) * SCALE)
        return weighted.astype(BF16), grad_score.astype(BF16)

    def put(span, unit, grad):
        grads_ref[span * SPAN : (span + 1) * SPAN, unit * HEAD_DIM : (unit + 1) * HEAD_DIM] = (
            grad.astype(BF16)
        )

    grad_k = None
    grad_v = None
    for span in range(GROUP):
        q, g, k, v = (unit_of(rows_ref, span, unit) for unit in range(4))
        here = slice(span * SPAN, (span + 1) * SPAN)
        if span == 0:
            k_front, v_front = unit_of(front_ref, 0, 0), unit_of(front_ref, 1, 0)
        else:
            k_front, v_front = unit_of(rows_ref, span - 1, 2), unit_of(rows_ref, span - 1, 3)
        row = (stats_ref[0:1, here], own[0][:, here], own[1][:, here])
        weight, scaled = graded(k, v, q, g, *row)
        weight_front, scaled_front = graded(k_front, v_front, q, g, *row)
        put(span, 0, dot_tn(scaled, k) + dot_tn(scaled_front, k_front))
        if span > 0:
            put(span - 1, 1, grad_k + dot(scaled_front, q))
            put(span - 1, 2, grad_v + dot(weight_front, g))
        grad_k = dot(scaled, q)
        grad_v = dot(weight, g)
    q, g = behind_ref[:SPAN, :HEAD_DIM], behind_ref[:SPAN, HEAD_DIM:]
    weight, scaled = graded(k, v, q, g, other[2], other[0], other[1])
    put(GROUP - 1, 1, grad_k + dot(scaled, q))
    put(GROUP - 1, 2, grad_v + dot(weight, g))
    wide = 3 * HEAD_DIM
    slot = source * SLOTS + slot
    for half in range(HALVES):
        here = slice(half * 2 * SPAN, (half + 1) * 2 * SPAN)
        for start in range(0, flat, SPAN):
            at = slot[:, here]
            across = hot_rows(jnp.where((at >= start) & (at < start + SPAN), at - start, -1))
            send_ref[start : start + SPAN, half * wide : (half + 1) * wide] = dot(
                across, grads_ref[here, :]
            ).astype(BF16)


def final_kernel(n, slots_ref, ret_ref, dq_ref, dk_ref, dv_ref):
    tall = n // GROUP * SLOTS
    both = ROUNDS * tall
    wide = 3 * HEAD_DIM
    slots = jnp.transpose(slots_ref[...].astype(F32)).astype(I32)
    at = iota((slots.shape[0], tall), 1)
    chosen = []
    for half in range(HALVES):
        for turn in range(ROUNDS):
            slot = slots[:, turn : turn + 1]
            row = (slot >> 4) * SLOTS + (slot & 7)
            chosen.append(hot(at == jnp.where(((slot >> 3) & 1) == half, row, -1)))
    chosen = [jnp.concatenate(chosen[i * 2 : i * 2 + 2], axis=1) for i in range(HALVES)]
    for head in range(dq_ref.shape[1] // HEAD_DIM):
        rows = slice(head * both, (head + 1) * both)
        total = dot(chosen[0], ret_ref[rows, :wide]) + dot(chosen[1], ret_ref[rows, wide:])
        for unit, ref in enumerate((dq_ref, dk_ref, dv_ref)):
            ref[:, head * HEAD_DIM : (head + 1) * HEAD_DIM] = total[
                :, unit * HEAD_DIM : (unit + 1) * HEAD_DIM
            ].astype(BF16)


def call(kernel, out, name, scratch=()):
    return pl.pallas_call(
        kernel,
        out_shape=out,
        scratch_shapes=scratch,
        name=name,
        compiler_params=pltpu.CompilerParams(vmem_limit_bytes=24 * 1024 * 1024),
    )


def shape(*dims, dtype=BF16):
    return jax.ShapeDtypeStruct(dims, dtype)


def exchanged(block):
    return lax.all_to_all(block, "seq", split_axis=0, concat_axis=0, tiled=True)


def from_next_group(block):
    n = lax.axis_size("seq")
    groups = n // GROUP
    route = [(i // groups * groups + (i + 1) % groups, i) for i in range(n)]
    return lax.ppermute(block, "seq", route)


def body(queries, keys, values, out_grad, sorted_position):
    n = lax.axis_size("seq")
    tokens, width = queries.shape
    heads = width // HEAD_DIM
    flat = n * SLOTS
    places = GROUP * SPAN
    placed = lax.all_gather(sorted_position, "head", axis=0, tiled=True)
    send, slots = call(
        functools.partial(pack_kernel, n),
        (shape(flat, (4 * HALVES + 1) * HEAD_DIM), shape(8, tokens, dtype=I32)),
        "pack",
    )(placed, jnp.concatenate([queries, out_grad, keys, values], axis=1))
    rows, front, first, info = call(
        functools.partial(unpack_kernel, n),
        (
            shape(places, 4 * HEAD_DIM),
            shape(2 * SPAN, HEAD_DIM),
            shape(SPAN + 16, 2 * HEAD_DIM),
            shape(8, places, dtype=F32),
        ),
        "unpack",
    )(exchanged(send))
    behind = from_next_group(first)
    table, stats = call(
        functools.partial(forward_kernel, n),
        (shape(n, LANES, dtype=F32), shape(8, places, dtype=F32)),
        "forward",
    )(rows, front, info)
    back = call(functools.partial(home_kernel, n, heads), shape(n, LANES, dtype=F32), "home")(
        exchanged(table), slots
    )
    grads = call(
        functools.partial(backward_kernel, n),
        shape(flat, 3 * HALVES * HEAD_DIM),
        "backward",
        [pltpu.VMEM((places, 3 * HEAD_DIM), BF16)],
    )(rows, front, behind, info, stats, exchanged(back))
    return call(functools.partial(final_kernel, n), (shape(tokens, width),) * 3, "final")(
        slots, exchanged(grads)
    )


def solution(mesh):
    in_specs = (
        P("seq", "head"),
        P("seq", "head"),
        P("seq", "head"),
        P("seq", "head"),
        P(None, ("seq", "head")),
    )
    out_specs = (P("seq", "head"), P("seq", "head"), P("seq", "head"))
    return jax.shard_map(body, mesh=mesh, in_specs=in_specs, out_specs=out_specs, check_vma=False)
```

```python
import functools
import math

import jax
import jax.numpy as jnp
from jax import lax
from jax.experimental import pallas as pl
from jax.experimental.pallas import tpu as pltpu
from jax.sharding import PartitionSpec as P

HEAD_DIM = 128
SPAN = 256
ROUNDS = 2
CAP = 4
GROUP = 4
SLOTS = 8
HALVES = 2
LANES = 128
DUP_LANE = 16
SOURCE_LANE = 20
NOTES = 24
SCALE = 1.0 / math.sqrt(HEAD_DIM)
F32 = jnp.float32
BF16 = jnp.bfloat16
I32 = jnp.int32


def iota(shape, dim):
    return lax.broadcasted_iota(I32, shape, dim)


def hot(condition):
    return jnp.where(condition, 1.0, 0.0).astype(BF16)


def dot(a, b):
    return lax.dot_general(a, b, (((1,), (0,)), ((), ())), preferred_element_type=F32)


def dot_nt(a, b):
    return lax.dot_general(a, b, (((1,), (1,)), ((), ())), preferred_element_type=F32)


def dot_tn(a, b):
    return lax.dot_general(a, b, (((0,), (0,)), ((), ())), preferred_element_type=F32)


def three_parts(x):
    high = x.astype(BF16).astype(F32)
    rest = x - high
    middle = rest.astype(BF16).astype(F32)
    return high, middle, (rest - middle).astype(BF16).astype(F32)


def picked(x, onehot, product):
    rows = x.shape[0]
    stacked = jnp.concatenate(three_parts(x), axis=0).astype(BF16)
    out = product(stacked, onehot)
    return out[:rows] + out[rows : 2 * rows] + out[2 * rows :]


def hot_rows(code, rows=SPAN):
    at = iota((rows, LANES), 0).astype(F32).astype(BF16)
    code = code.astype(F32).astype(BF16)
    pieces = [
        jnp.where(at == code[:, i : i + LANES], jnp.ones_like(at), jnp.zeros_like(at))
        for i in range(0, code.shape[1], LANES)
    ]
    return jnp.concatenate(pieces, axis=1)


def pack_kernel(n, pos_ref, held_ref, send_ref, slots_ref):
    tokens = held_ref.shape[0]
    width = held_ref.shape[1] // 4
    heads = width // HEAD_DIM
    quarters = pos_ref.shape[0] // ROUNDS
    tall = n // GROUP * SLOTS
    before = hot(iota((tokens, tokens), 0) < iota((tokens, tokens), 1))
    main = [[], []]
    edge = []
    notes = []
    slots = []
    all_places = [
        jnp.concatenate(
            [pos_ref[x * ROUNDS + turn : x * ROUNDS + turn + 1, :] for x in range(quarters)], axis=1
        )
        for turn in range(ROUNDS)
    ]
    lane = iota((LANES, tokens), 0)
    for turn in range(ROUNDS):
        places = all_places[turn]
        other = all_places[1 - turn]
        span = places >> 8
        inner = span & 3
        member = hot_rows(span, n)
        earlier = dot(member, before)
        rank = jnp.sum(member.astype(F32) * earlier, axis=0, keepdims=True).astype(I32)
        slots.append(span * CAP + rank)
        row = (span >> 2) * SLOTS + rank
        for half in range(HALVES):
            here = (inner >> 1) == half
            main[half].append(hot_rows(jnp.where(here, row + (inner & 1) * CAP, -1)))
        last = (span & 7) == 7
        first = (((span + 1) & (n - 1)) >> 2) * SLOTS + rank
        edge.append([hot_rows(jnp.where(last, first + i * SLOTS, -1)) for i in range(2)])
        landing = (places & 255) + 1
        values = jnp.where(lane == inner * 4, landing, 0)
        values = jnp.where(lane == inner * 4 + 1, other >> 7, values)
        values = jnp.where(lane == inner * 4 + 2, other & 127, values)
        note = dot_nt(hot_rows(row + CAP), values.astype(F32).astype(BF16))
        values = jnp.where(lane == DUP_LANE, landing, 0).astype(F32).astype(BF16)
        both = [hot_rows(jnp.where(last, first + i * SLOTS + CAP, -1)) for i in range(2)]
        notes.append(note + dot_nt(both[0] + both[1], values))
    slots_ref[...] = jnp.concatenate(slots + [jnp.zeros((8 - ROUNDS, tokens), I32)], axis=0)
    chosen = jnp.concatenate(main[0] + main[1], axis=0)

    def store(column, part):
        for head in range(heads):
            rows = slice(head * ROUNDS * tall, (head + 1) * ROUNDS * tall)
            send_ref[rows, column * HEAD_DIM : (column + 1) * HEAD_DIM] = part[
                :, head * HEAD_DIM : (head + 1) * HEAD_DIM
            ].astype(BF16)

    both = ROUNDS * tall
    for unit in range(4):
        part = dot(chosen, held_ref[:, unit * width : (unit + 1) * width])
        for half in range(HALVES):
            store(half * 4 + unit, part[half * both : (half + 1) * both])
    extra = dot(jnp.concatenate([edge[0][0], edge[1][0]], axis=0), held_ref[:, 2 * width : 3 * width])
    extra = extra + dot(
        jnp.concatenate([edge[0][1], edge[1][1]], axis=0), held_ref[:, 3 * width :]
    )
    notes = jnp.concatenate(notes, axis=0)
    store(HALVES * 4, extra + jnp.concatenate([notes] * heads, axis=1))


def unpack_kernel(n, me_ref, recv_ref, rows_ref, dup_ref, pair_ref, head_ref, info_ref):
    flat = n * SLOTS
    wide = 4 * HEAD_DIM
    odd = (me_ref[0] & 1) == 1
    extra = recv_ref[:, HALVES * wide :]
    at = iota((flat, LANES), 0)
    lane = iota((flat, LANES), 1)
    notes = extra.astype(F32)
    notes = jnp.where((at & 7) < CAP, pltpu.roll(notes, flat - CAP, 0), notes)
    notes = jnp.where(lane == SOURCE_LANE, (at >> 3).astype(F32), notes)
    notes = jnp.where(lane == SOURCE_LANE + 1, (at & 7).astype(F32), notes).astype(BF16)
    by_slot = dot_nt(hot(iota((NOTES, LANES), 0) == iota((NOTES, LANES), 1)), notes).astype(I32)
    upper = (iota((1, flat), 1) & 7) >= CAP
    for half in range(HALVES):
        here = slice(half * 2 * SPAN, (half + 1) * 2 * SPAN)
        chosen = []
        for i in range(2):
            row = (half * 2 + i) * 4
            chosen.append(hot_rows(jnp.where(upper == (i == 1), by_slot[row : row + 1] - 1, -1)))
        chosen = jnp.concatenate(chosen, axis=0)
        rows = dot(chosen, recv_ref[:, half * wide : (half + 1) * wide]).astype(BF16)
        rows_ref[here, :] = rows
        by_place = jnp.transpose(dot(chosen, notes))[:NOTES]
        row = half * 8
        away = [
            jnp.concatenate(
                [by_place[row + i : row + i + 1, :SPAN], by_place[row + i + 4 : row + i + 5, SPAN:]],
                axis=1,
            )
            for i in (1, 2)
        ]
        info = jnp.concatenate(
            away
            + [by_place[SOURCE_LANE : SOURCE_LANE + 2], jnp.zeros((4, 2 * SPAN), F32)],
            axis=0,
        )
        info_ref[:, here] = info
        if half == 0:
            head_ref[:SPAN, :] = rows[:SPAN, : 2 * HEAD_DIM]
            head_ref[SPAN:, :] = jnp.concatenate(
                [info[:, :SPAN], jnp.zeros((8, SPAN), F32)], axis=0
            ).astype(BF16)
    chosen = hot_rows(jnp.where(upper, -1, by_slot[DUP_LANE : DUP_LANE + 1] - 1))
    dup = dot(chosen, extra)
    dup_ref[...] = dup.astype(BF16)
    dup = jnp.concatenate([dup, jnp.zeros_like(dup)], axis=1)
    last = rows_ref[(GROUP - 1) * SPAN :, 2 * HEAD_DIM :].astype(F32)
    pair_ref[...] = jnp.where(odd, dup, last).astype(BF16)


def before_group(odd, dup_ref, pair_ref):
    k_even, v_even = pair_ref[:SPAN, :HEAD_DIM], pair_ref[:SPAN, HEAD_DIM:]
    k_front = jnp.where(odd, k_even.astype(F32), dup_ref[...].astype(F32))
    v_front = jnp.where(odd, v_even.astype(F32), pair_ref[SPAN:, :HEAD_DIM].astype(F32))
    return k_front.astype(BF16), v_front.astype(BF16)


def unit_of(ref, span, unit):
    return ref[span * SPAN : (span + 1) * SPAN, unit * HEAD_DIM : (unit + 1) * HEAD_DIM]


def forward_kernel(me_ref, rows_ref, dup_ref, pair_ref, table_ref, stats_ref):
    front = before_group((me_ref[0] & 1) == 1, dup_ref, pair_ref)
    for span in range(GROUP):
        q, g, k, v = (unit_of(rows_ref, span, unit) for unit in range(4))
        if span == 0:
            k_front, v_front = front
        else:
            k_front, v_front = unit_of(rows_ref, span - 1, 2), unit_of(rows_ref, span - 1, 3)
        score = dot_nt(k, q) * SCALE
        score_front = dot_nt(k_front, q) * SCALE
        highest = jnp.maximum(
            jnp.max(score, axis=0, keepdims=True), jnp.max(score_front, axis=0, keepdims=True)
        )
        raised = jnp.exp(score - highest)
        raised_front = jnp.exp(score_front - highest)
        total = jnp.sum(raised + raised_front, axis=0, keepdims=True)
        mixed = jnp.sum(
            raised * dot_nt(v, g) + raised_front * dot_nt(v_front, g), axis=0, keepdims=True
        )
        here = slice(span * SPAN, (span + 1) * SPAN)
        for kind, row in enumerate((highest + jnp.log(total), mixed / total)):
            stats_ref[kind : kind + 1, here] = row
            for i in range(2):
                at = kind * SLOTS + span * 2 + i
                table_ref[at : at + 1, :] = row[:, i * LANES : (i + 1) * LANES]
    stats_ref[2:, :] = jnp.zeros((6, GROUP * SPAN), F32)


def backward_kernel(
    n,
    me_ref,
    rows_ref,
    dup_ref,
    pair_ref,
    behind_ref,
    info_ref,
    stats_ref,
    table_ref,
    send_ref,
    grads_ref,
):
    flat = n * SLOTS
    groups = n // GROUP
    me = me_ref[0]
    turn = (me >> 5) & 1
    group = (me + 1) & (groups - 1)
    behind_info = behind_ref[SPAN : SPAN + 8, :].astype(F32)
    far = jnp.concatenate([info_ref[0:1, :], behind_info[0:1]], axis=1).astype(I32)
    near = jnp.concatenate([info_ref[1:2, :], behind_info[1:2]], axis=1).astype(I32)
    chosen = hot_rows(((far >> 3) & 15) * 16 + (far >> 7) * 8 + (far & 7))
    keep = iota((LANES, far.shape[1]), 0) == near

    def tile(turn, high, kind):
        return pl.ds(pl.multiple_of(turn * 32 + high * 16 + kind * 8, 8), 8)

    there = []
    own = []
    for kind in range(2):
        tiles = [table_ref[:, tile(1 - turn, high, kind), :] for high in range(2)]
        there.append(jnp.transpose(jnp.concatenate(tiles, axis=1).reshape(2 * LANES, LANES)))
        next_tile = table_ref[group & 15, tile(turn, group >> 4, kind), :]
        own.append(
            jnp.concatenate([stats_ref[kind : kind + 1, :], next_tile[0:1], next_tile[1:2]], axis=1)
        )
    found = picked(jnp.concatenate(there, axis=0), chosen, dot)
    other = [
        jnp.sum(
            jnp.where(keep, found[kind * LANES : (kind + 1) * LANES], 0.0), axis=0, keepdims=True
        )
        for kind in range(2)
    ]
    highest = jnp.maximum(own[0], other[0])
    raised = jnp.exp(own[0] - highest)
    raised_other = jnp.exp(other[0] - highest)
    total = raised + raised_other
    shares = raised / total
    means = (raised * own[1] + raised_other * other[1]) / total

    def graded(keys, vals, queries, grads, log_total, share, mean):
        weighted = jnp.exp(dot_nt(keys, queries) * SCALE - log_total) * share
        grad_score = weighted * ((dot_nt(vals, grads) - mean) * SCALE)
        return weighted.astype(BF16), grad_score.astype(BF16)

    def put(span, unit, grad):
        grads_ref[span * SPAN : (span + 1) * SPAN, unit * HEAD_DIM : (unit + 1) * HEAD_DIM] = (
            grad.astype(BF16)
        )

    grad_k = None
    grad_v = None
    for span in range(GROUP):
        q, g, k, v = (unit_of(rows_ref, span, unit) for unit in range(4))
        here = slice(span * SPAN, (span + 1) * SPAN)
        if span == 0:
            k_front, v_front = before_group((me & 1) == 1, dup_ref, pair_ref)
        else:
            k_front, v_front = unit_of(rows_ref, span - 1, 2), unit_of(rows_ref, span - 1, 3)
        row = (own[0][:, here], shares[:, here], means[:, here])
        weight, scaled = graded(k, v, q, g, *row)
        weight_front, scaled_front = graded(k_front, v_front, q, g, *row)
        put(span, 0, dot_tn(scaled, k) + dot_tn(scaled_front, k_front))
        if span > 0:
            put(span - 1, 1, grad_k + dot(scaled_front, q))
            put(span - 1, 2, grad_v + dot(weight_front, g))
        grad_k = dot(scaled, q)
        grad_v = dot(weight, g)
    here = slice(GROUP * SPAN, (GROUP + 1) * SPAN)
    q, g = behind_ref[:SPAN, :HEAD_DIM], behind_ref[:SPAN, HEAD_DIM:]
    weight, scaled = graded(k, v, q, g, own[0][:, here], shares[:, here], means[:, here])
    put(GROUP - 1, 1, grad_k + dot(scaled, q))
    put(GROUP - 1, 2, grad_v + dot(weight, g))
    wide = 3 * HEAD_DIM
    slot = (info_ref[2:3, :] * SLOTS + info_ref[3:4, :]).astype(I32)
    for half in range(HALVES):
        here = slice(half * 2 * SPAN, (half + 1) * 2 * SPAN)
        for start in range(0, flat, SPAN):
            at = slot[:, here]
            across = hot_rows(jnp.where((at >= start) & (at < start + SPAN), at - start, -1))
            send_ref[start : start + SPAN, half * wide : (half + 1) * wide] = dot(
                across, grads_ref[here, :]
            ).astype(BF16)


def final_kernel(n, slots_ref, ret_ref, dq_ref, dk_ref, dv_ref):
    tall = n // GROUP * SLOTS
    both = ROUNDS * tall
    wide = 3 * HEAD_DIM
    slots = jnp.transpose(slots_ref[...].astype(F32)).astype(I32)
    at = iota((slots.shape[0], tall), 1)
    chosen = []
    for half in range(HALVES):
        for turn in range(ROUNDS):
            slot = slots[:, turn : turn + 1]
            row = (slot >> 4) * SLOTS + (slot & 7)
            chosen.append(hot(at == jnp.where(((slot >> 3) & 1) == half, row, -1)))
    chosen = [jnp.concatenate(chosen[i * 2 : i * 2 + 2], axis=1) for i in range(HALVES)]
    for head in range(dq_ref.shape[1] // HEAD_DIM):
        rows = slice(head * both, (head + 1) * both)
        total = dot(chosen[0], ret_ref[rows, :wide]) + dot(chosen[1], ret_ref[rows, wide:])
        for unit, ref in enumerate((dq_ref, dk_ref, dv_ref)):
            ref[:, head * HEAD_DIM : (head + 1) * HEAD_DIM] = total[
                :, unit * HEAD_DIM : (unit + 1) * HEAD_DIM
            ].astype(BF16)


def call(kernel, out, name, args, scratch=()):
    where = [pltpu.SMEM if x.shape == (1,) else pltpu.VMEM for x in args]
    return pl.pallas_call(
        kernel,
        out_shape=out,
        in_specs=[pl.BlockSpec(memory_space=space) for space in where],
        scratch_shapes=scratch,
        name=name,
        compiler_params=pltpu.CompilerParams(vmem_limit_bytes=24 * 1024 * 1024),
    )(*args)


def shape(*dims, dtype=BF16):
    return jax.ShapeDtypeStruct(dims, dtype)


def exchanged(block):
    return lax.all_to_all(block, "seq", split_axis=0, concat_axis=0, tiled=True)


def gathered(block, members):
    n = lax.axis_size("seq")
    taken = set()
    groups = []
    for first in range(n):
        if first not in taken:
            groups.append([first + offset for offset in members])
            taken.update(groups[-1])
    return lax.all_gather(block, "seq", axis=0, tiled=True, axis_index_groups=groups)


def from_next_group(block):
    n = lax.axis_size("seq")
    groups = n // GROUP
    route = [(i // groups * groups + (i + 1) % groups, i) for i in range(n)]
    return lax.ppermute(block, "seq", route)


def body(queries, keys, values, out_grad, sorted_position):
    n = lax.axis_size("seq")
    tokens, width = queries.shape
    flat = n * SLOTS
    places = GROUP * SPAN
    me = lax.axis_index("seq").astype(I32).reshape(1)
    placed = lax.all_gather(sorted_position, "head", axis=0, tiled=True)
    send, slots = call(
        functools.partial(pack_kernel, n),
        (shape(flat, (4 * HALVES + 1) * HEAD_DIM), shape(8, tokens, dtype=I32)),
        "pack",
        (placed, jnp.concatenate([queries, out_grad, keys, values], axis=1)),
    )
    send, me = lax.optimization_barrier((send, me))
    rows, dup, last, first, info = call(
        functools.partial(unpack_kernel, n),
        (
            shape(places, 4 * HEAD_DIM),
            shape(SPAN, HEAD_DIM),
            shape(SPAN, 2 * HEAD_DIM),
            shape(SPAN + 16, 2 * HEAD_DIM),
            shape(8, places, dtype=F32),
        ),
        "unpack",
        (me, exchanged(send)),
    )
    behind = from_next_group(first)
    pair = gathered(last, (0, 1))
    table, stats = call(
        forward_kernel,
        (shape(2 * SLOTS, LANES, dtype=F32), shape(8, places, dtype=F32)),
        "forward",
        (me, rows, dup, pair),
    )
    for members in ((0, n // 8), (0, n // 4), range(n // 8)):
        table = gathered(table, members)
    grads = call(
        functools.partial(backward_kernel, n),
        shape(flat, 3 * HALVES * HEAD_DIM),
        "backward",
        (me, rows, dup, pair, behind, info, stats, table.reshape(n // 8, 4 * 2 * SLOTS, LANES)),
        [pltpu.VMEM((places, 3 * HEAD_DIM), BF16)],
    )
    return call(
        functools.partial(final_kernel, n),
        (shape(tokens, width),) * 3,
        "final",
        (slots, exchanged(grads)),
    )


def solution(mesh):
    in_specs = (
        P("seq", "head"),
        P("seq", "head"),
        P("seq", "head"),
        P("seq", "head"),
        P(None, ("seq", "head")),
    )
    out_specs = (P("seq", "head"), P("seq", "head"), P("seq", "head"))
    return jax.shard_map(body, mesh=mesh, in_specs=in_specs, out_specs=out_specs, check_vma=False)
```

```python
import functools
import math

import jax
import jax.numpy as jnp
from jax import lax
from jax.experimental import pallas as pl
from jax.experimental.pallas import tpu as pltpu
from jax.sharding import PartitionSpec as P

HEAD_DIM = 128
SPAN = 256
ROUNDS = 2
CAP = 4
GROUP = 4
SLOTS = 8
HALVES = 2
LANES = 128
DUP_LANE = 16
SOURCE_LANE = 20
NOTES = 24
SCALE = 1.0 / math.sqrt(HEAD_DIM)
F32 = jnp.float32
BF16 = jnp.bfloat16
I32 = jnp.int32


def iota(shape, dim):
    return lax.broadcasted_iota(I32, shape, dim)


def hot(condition):
    return jnp.where(condition, 1.0, 0.0).astype(BF16)


def dot(a, b):
    return lax.dot_general(a, b, (((1,), (0,)), ((), ())), preferred_element_type=F32)


def dot_nt(a, b):
    return lax.dot_general(a, b, (((1,), (1,)), ((), ())), preferred_element_type=F32)


def dot_tn(a, b):
    return lax.dot_general(a, b, (((0,), (0,)), ((), ())), preferred_element_type=F32)


def three_parts(x):
    high = x.astype(BF16).astype(F32)
    rest = x - high
    middle = rest.astype(BF16).astype(F32)
    return high, middle, (rest - middle).astype(BF16).astype(F32)


def picked(x, onehot, product):
    rows = x.shape[0]
    stacked = jnp.concatenate(three_parts(x), axis=0).astype(BF16)
    out = product(stacked, onehot)
    return out[:rows] + out[rows : 2 * rows] + out[2 * rows :]


def hot_rows(code, rows=SPAN):
    at = iota((rows, LANES), 0).astype(F32).astype(BF16)
    code = code.astype(F32).astype(BF16)
    pieces = [
        jnp.where(at == code[:, i : i + LANES], jnp.ones_like(at), jnp.zeros_like(at))
        for i in range(0, code.shape[1], LANES)
    ]
    return jnp.concatenate(pieces, axis=1)


def pack_kernel(n, pos_ref, held_ref, send_ref, slots_ref):
    tokens = held_ref.shape[0]
    width = held_ref.shape[1] // 4
    heads = width // HEAD_DIM
    quarters = pos_ref.shape[0] // ROUNDS
    tall = n // GROUP * SLOTS
    before = hot(iota((tokens, tokens), 0) < iota((tokens, tokens), 1))
    main = [[], []]
    edge = []
    notes = []
    slots = []
    all_places = [
        jnp.concatenate(
            [pos_ref[x * ROUNDS + turn : x * ROUNDS + turn + 1, :] for x in range(quarters)], axis=1
        )
        for turn in range(ROUNDS)
    ]
    lane = iota((LANES, tokens), 0)
    for turn in range(ROUNDS):
        places = all_places[turn]
        other = all_places[1 - turn]
        span = places >> 8
        inner = span & 3
        member = hot_rows(span, n)
        earlier = dot(member, before)
        rank = jnp.sum(member.astype(F32) * earlier, axis=0, keepdims=True).astype(I32)
        slots.append(span * CAP + rank)
        row = (span >> 2) * SLOTS + rank
        for half in range(HALVES):
            here = (inner >> 1) == half
            main[half].append(hot_rows(jnp.where(here, row + (inner & 1) * CAP, -1)))
        last = (span & 7) == 7
        first = (((span + 1) & (n - 1)) >> 2) * SLOTS + rank
        edge.append([hot_rows(jnp.where(last, first + i * SLOTS, -1)) for i in range(2)])
        landing = (places & 255) + 1
        values = jnp.where(lane == inner * 4, landing, 0)
        values = jnp.where(lane == inner * 4 + 1, other >> 7, values)
        values = jnp.where(lane == inner * 4 + 2, other & 127, values)
        note = dot_nt(hot_rows(row + CAP), values.astype(F32).astype(BF16))
        values = jnp.where(lane == DUP_LANE, landing, 0).astype(F32).astype(BF16)
        both = [hot_rows(jnp.where(last, first + i * SLOTS + CAP, -1)) for i in range(2)]
        notes.append(note + dot_nt(both[0] + both[1], values))
    slots_ref[...] = jnp.concatenate(slots + [jnp.zeros((8 - ROUNDS, tokens), I32)], axis=0)
    chosen = jnp.concatenate(main[0] + main[1], axis=0)

    def store(column, part):
        for head in range(heads):
            rows = slice(head * ROUNDS * tall, (head + 1) * ROUNDS * tall)
            send_ref[rows, column * HEAD_DIM : (column + 1) * HEAD_DIM] = part[
                :, head * HEAD_DIM : (head + 1) * HEAD_DIM
            ].astype(BF16)

    both = ROUNDS * tall
    for unit in range(4):
        part = dot(chosen, held_ref[:, unit * width : (unit + 1) * width])
        for half in range(HALVES):
            store(half * 4 + unit, part[half * both : (half + 1) * both])
    extra = dot(jnp.concatenate([edge[0][0], edge[1][0]], axis=0), held_ref[:, 2 * width : 3 * width])
    extra = extra + dot(
        jnp.concatenate([edge[0][1], edge[1][1]], axis=0), held_ref[:, 3 * width :]
    )
    notes = jnp.concatenate(notes, axis=0)
    store(HALVES * 4, extra + jnp.concatenate([notes] * heads, axis=1))


def unpack_kernel(n, me_ref, recv_ref, rows_ref, dup_ref, pair_ref, head_ref, info_ref):
    flat = n * SLOTS
    wide = 4 * HEAD_DIM
    odd = (me_ref[0] & 1) == 1
    extra = recv_ref[:, HALVES * wide :]
    at = iota((flat, LANES), 0)
    lane = iota((flat, LANES), 1)
    notes = extra.astype(F32)
    notes = jnp.where((at & 7) < CAP, pltpu.roll(notes, flat - CAP, 0), notes)
    notes = jnp.where(lane == SOURCE_LANE, (at >> 3).astype(F32), notes)
    notes = jnp.where(lane == SOURCE_LANE + 1, (at & 7).astype(F32), notes).astype(BF16)
    by_slot = dot_nt(hot(iota((NOTES, LANES), 0) == iota((NOTES, LANES), 1)), notes).astype(I32)
    upper = (iota((1, flat), 1) & 7) >= CAP
    for half in range(HALVES):
        here = slice(half * 2 * SPAN, (half + 1) * 2 * SPAN)
        chosen = []
        for i in range(2):
            row = (half * 2 + i) * 4
            chosen.append(hot_rows(jnp.where(upper == (i == 1), by_slot[row : row + 1] - 1, -1)))
        chosen = jnp.concatenate(chosen, axis=0)
        rows = dot(chosen, recv_ref[:, half * wide : (half + 1) * wide]).astype(BF16)
        rows_ref[here, :] = rows
        by_place = jnp.transpose(dot(chosen, notes))[:NOTES]
        row = half * 8
        away = [
            jnp.concatenate(
                [by_place[row + i : row + i + 1, :SPAN], by_place[row + i + 4 : row + i + 5, SPAN:]],
                axis=1,
            )
            for i in (1, 2)
        ]
        info = jnp.concatenate(
            away
            + [by_place[SOURCE_LANE : SOURCE_LANE + 2], jnp.zeros((4, 2 * SPAN), F32)],
            axis=0,
        )
        info_ref[:, here] = info
        if half == 0:
            head_ref[:SPAN, :] = rows[:SPAN, : 2 * HEAD_DIM]
            head_ref[SPAN:, :] = jnp.concatenate(
                [info[:, :SPAN], jnp.zeros((8, SPAN), F32)], axis=0
            ).astype(BF16)
    chosen = hot_rows(jnp.where(upper, -1, by_slot[DUP_LANE : DUP_LANE + 1] - 1))
    dup = dot(chosen, extra)
    dup_ref[...] = dup.astype(BF16)
    dup = jnp.concatenate([dup, jnp.zeros_like(dup)], axis=1)
    last = rows_ref[(GROUP - 1) * SPAN :, 2 * HEAD_DIM :].astype(F32)
    pair_ref[...] = jnp.where(odd, dup, last).astype(BF16)


def before_group(odd, dup_ref, pair_ref):
    k_even, v_even = pair_ref[:SPAN, :HEAD_DIM], pair_ref[:SPAN, HEAD_DIM:]
    k_front = jnp.where(odd, k_even.astype(F32), dup_ref[...].astype(F32))
    v_front = jnp.where(odd, v_even.astype(F32), pair_ref[SPAN:, :HEAD_DIM].astype(F32))
    return k_front.astype(BF16), v_front.astype(BF16)


def unit_of(ref, span, unit):
    return ref[span * SPAN : (span + 1) * SPAN, unit * HEAD_DIM : (unit + 1) * HEAD_DIM]


def forward_kernel(me_ref, rows_ref, dup_ref, pair_ref, table_ref, stats_ref, tile_ref):
    front = before_group((me_ref[0] & 1) == 1, dup_ref, pair_ref)
    for span in range(GROUP):
        q, g, k, v = (unit_of(rows_ref, span, unit) for unit in range(4))
        if span == 0:
            k_front, v_front = front
        else:
            k_front, v_front = unit_of(rows_ref, span - 1, 2), unit_of(rows_ref, span - 1, 3)
        score = dot_nt(k, q) * SCALE
        score_front = dot_nt(k_front, q) * SCALE
        highest = jnp.maximum(
            jnp.max(score, axis=0, keepdims=True), jnp.max(score_front, axis=0, keepdims=True)
        )
        raised = jnp.exp(score - highest)
        raised_front = jnp.exp(score_front - highest)
        total = jnp.sum(raised + raised_front, axis=0, keepdims=True)
        mixed = jnp.sum(
            raised * dot_nt(v, g) + raised_front * dot_nt(v_front, g), axis=0, keepdims=True
        )
        here = slice(span * SPAN, (span + 1) * SPAN)
        log_total = highest + jnp.log(total)
        high = log_total.astype(BF16).astype(F32)
        rows = (high, log_total - high, mixed / total)
        for kind, row in enumerate(rows):
            for i in range(2):
                at = kind * 2 * GROUP + span * 2 + i
                tile_ref[at : at + 1, :] = row[:, i * LANES : (i + 1) * LANES]
        stats_ref[0:1, here] = log_total
        stats_ref[1:2, here] = rows[2]
    stats_ref[2:, :] = jnp.zeros((6, GROUP * SPAN), F32)
    table_ref[...] = jnp.broadcast_to(tile_ref[...].astype(BF16)[None], table_ref.shape)


def backward_kernel(
    n,
    me_ref,
    rows_ref,
    dup_ref,
    pair_ref,
    behind_ref,
    info_ref,
    stats_ref,
    table_ref,
    send_ref,
    grads_ref,
):
    flat = n * SLOTS
    groups = n // GROUP
    me = me_ref[0]
    turn = (me >> 5) & 1
    group = (me + 1) & (groups - 1)
    behind_info = behind_ref[SPAN : SPAN + 8, :].astype(F32)
    far = jnp.concatenate([info_ref[0:1, :], behind_info[0:1]], axis=1).astype(I32)
    near = jnp.concatenate([info_ref[1:2, :], behind_info[1:2]], axis=1).astype(I32)
    chosen = hot_rows(far)
    keep = iota((LANES, far.shape[1]), 0) == near

    there = table_ref[pl.ds(pl.multiple_of((1 - turn) * groups, groups), groups)].astype(F32)
    there = [
        jnp.transpose(there[:, kind * 8 : (kind + 1) * 8, :].reshape(groups * 8, LANES))
        for kind in range(3)
    ]
    found = dot(jnp.concatenate(there, axis=0).astype(BF16), chosen)
    other = [
        jnp.sum(jnp.where(keep, values, 0.0), axis=0, keepdims=True)
        for values in (found[:LANES] + found[LANES : 2 * LANES], found[2 * LANES :])
    ]
    tile = table_ref[turn * groups + group].astype(F32)
    tiles = (tile[0:8] + tile[8:16], tile[16:24])
    own = [
        jnp.concatenate([stats_ref[kind : kind + 1, :], tiles[kind][0:1], tiles[kind][1:2]], axis=1)
        for kind in range(2)
    ]
    highest = jnp.maximum(own[0], other[0])
    raised = jnp.exp(own[0] - highest)
    raised_other = jnp.exp(other[0] - highest)
    total = raised + raised_other
    shares = raised / total
    means = (raised * own[1] + raised_other * other[1]) / total

    def graded(keys, vals, queries, grads, log_total, share, mean):
        weighted = jnp.exp(dot_nt(keys, queries) * SCALE - log_total) * share
        grad_score = weighted * ((dot_nt(vals, grads) - mean) * SCALE)
        return weighted.astype(BF16), grad_score.astype(BF16)

    def put(span, unit, grad):
        grads_ref[span * SPAN : (span + 1) * SPAN, unit * HEAD_DIM : (unit + 1) * HEAD_DIM] = (
            grad.astype(BF16)
        )

    grad_k = None
    grad_v = None
    for span in range(GROUP):
        q, g, k, v = (unit_of(rows_ref, span, unit) for unit in range(4))
        here = slice(span * SPAN, (span + 1) * SPAN)
        if span == 0:
            k_front, v_front = before_group((me & 1) == 1, dup_ref, pair_ref)
        else:
            k_front, v_front = unit_of(rows_ref, span - 1, 2), unit_of(rows_ref, span - 1, 3)
        row = (own[0][:, here], shares[:, here], means[:, here])
        weight, scaled = graded(k, v, q, g, *row)
        weight_front, scaled_front = graded(k_front, v_front, q, g, *row)
        put(span, 0, dot_tn(scaled, k) + dot_tn(scaled_front, k_front))
        if span > 0:
            put(span - 1, 1, grad_k + dot(scaled_front, q))
            put(span - 1, 2, grad_v + dot(weight_front, g))
        grad_k = dot(scaled, q)
        grad_v = dot(weight, g)
    here = slice(GROUP * SPAN, (GROUP + 1) * SPAN)
    q, g = behind_ref[:SPAN, :HEAD_DIM], behind_ref[:SPAN, HEAD_DIM:]
    weight, scaled = graded(k, v, q, g, own[0][:, here], shares[:, here], means[:, here])
    put(GROUP - 1, 1, grad_k + dot(scaled, q))
    put(GROUP - 1, 2, grad_v + dot(weight, g))
    wide = 3 * HEAD_DIM
    slot = (info_ref[2:3, :] * SLOTS + info_ref[3:4, :]).astype(I32)
    for half in range(HALVES):
        here = slice(half * 2 * SPAN, (half + 1) * 2 * SPAN)
        for start in range(0, flat, SPAN):
            at = slot[:, here]
            across = hot_rows(jnp.where((at >= start) & (at < start + SPAN), at - start, -1))
            send_ref[start : start + SPAN, half * wide : (half + 1) * wide] = dot(
                across, grads_ref[here, :]
            ).astype(BF16)


def final_kernel(n, slots_ref, ret_ref, dq_ref, dk_ref, dv_ref):
    tall = n // GROUP * SLOTS
    both = ROUNDS * tall
    wide = 3 * HEAD_DIM
    slots = jnp.transpose(slots_ref[...].astype(F32)).astype(I32)
    at = iota((slots.shape[0], tall), 1)
    chosen = []
    for half in range(HALVES):
        for turn in range(ROUNDS):
            slot = slots[:, turn : turn + 1]
            row = (slot >> 4) * SLOTS + (slot & 7)
            chosen.append(hot(at == jnp.where(((slot >> 3) & 1) == half, row, -1)))
    chosen = [jnp.concatenate(chosen[i * 2 : i * 2 + 2], axis=1) for i in range(HALVES)]
    for head in range(dq_ref.shape[1] // HEAD_DIM):
        rows = slice(head * both, (head + 1) * both)
        total = dot(chosen[0], ret_ref[rows, :wide]) + dot(chosen[1], ret_ref[rows, wide:])
        for unit, ref in enumerate((dq_ref, dk_ref, dv_ref)):
            ref[:, head * HEAD_DIM : (head + 1) * HEAD_DIM] = total[
                :, unit * HEAD_DIM : (unit + 1) * HEAD_DIM
            ].astype(BF16)


def call(kernel, out, name, args, scratch=()):
    where = [pltpu.SMEM if x.shape == (1,) else pltpu.VMEM for x in args]
    return pl.pallas_call(
        kernel,
        out_shape=out,
        in_specs=[pl.BlockSpec(memory_space=space) for space in where],
        scratch_shapes=scratch,
        name=name,
        compiler_params=pltpu.CompilerParams(vmem_limit_bytes=24 * 1024 * 1024),
    )(*args)


def shape(*dims, dtype=BF16):
    return jax.ShapeDtypeStruct(dims, dtype)


def exchanged(block):
    return lax.all_to_all(block, "seq", split_axis=0, concat_axis=0, tiled=True)


def pair_gathered(block):
    n = lax.axis_size("seq")
    groups = [[i, i + 1] for i in range(0, n, 2)]
    return lax.all_gather(block, "seq", axis=0, tiled=True, axis_index_groups=groups)


def head_exchanged(block):
    n = lax.axis_size("seq")
    groups = [list(range(i, i + n // 2)) for i in (0, n // 2)]
    return lax.all_to_all(
        block, "seq", split_axis=0, concat_axis=0, tiled=True, axis_index_groups=groups
    )


def from_next_group(block):
    n = lax.axis_size("seq")
    groups = n // GROUP
    route = [(i // groups * groups + (i + 1) % groups, i) for i in range(n)]
    return lax.ppermute(block, "seq", route)


def body(queries, keys, values, out_grad, sorted_position):
    n = lax.axis_size("seq")
    tokens, width = queries.shape
    flat = n * SLOTS
    places = GROUP * SPAN
    me = lax.axis_index("seq").astype(I32).reshape(1)
    placed = lax.all_gather(sorted_position, "head", axis=0, tiled=True)
    send, slots = call(
        functools.partial(pack_kernel, n),
        (shape(flat, (4 * HALVES + 1) * HEAD_DIM), shape(8, tokens, dtype=I32)),
        "pack",
        (placed, jnp.concatenate([queries, out_grad, keys, values], axis=1)),
    )
    send, me = lax.optimization_barrier((send, me))
    rows, dup, last, first, info = call(
        functools.partial(unpack_kernel, n),
        (
            shape(places, 4 * HEAD_DIM),
            shape(SPAN, HEAD_DIM),
            shape(SPAN, 2 * HEAD_DIM),
            shape(SPAN + 16, 2 * HEAD_DIM),
            shape(8, places, dtype=F32),
        ),
        "unpack",
        (me, exchanged(send)),
    )
    behind = from_next_group(first)
    pair = pair_gathered(last)
    table, stats = call(
        forward_kernel,
        (shape(n // 2, 3 * 2 * GROUP, LANES), shape(8, places, dtype=F32)),
        "forward",
        (me, rows, dup, pair),
        [pltpu.VMEM((3 * 2 * GROUP, LANES), F32)],
    )
    grads = call(
        functools.partial(backward_kernel, n),
        shape(flat, 3 * HALVES * HEAD_DIM),
        "backward",
        (me, rows, dup, pair, behind, info, stats, head_exchanged(table)),
        [pltpu.VMEM((places, 3 * HEAD_DIM), BF16)],
    )
    return call(
        functools.partial(final_kernel, n),
        (shape(tokens, width),) * 3,
        "final",
        (slots, exchanged(grads)),
    )


def solution(mesh):
    in_specs = (
        P("seq", "head"),
        P("seq", "head"),
        P("seq", "head"),
        P("seq", "head"),
        P(None, ("seq", "head")),
    )
    out_specs = (P("seq", "head"), P("seq", "head"), P("seq", "head"))
    return jax.shard_map(body, mesh=mesh, in_specs=in_specs, out_specs=out_specs, check_vma=False)
```

```python
import functools
import math

import jax
import jax.numpy as jnp
from jax import lax
from jax.experimental import pallas as pl
from jax.experimental.pallas import tpu as pltpu
from jax.sharding import PartitionSpec as P

HEAD_DIM = 128
SPAN = 256
ROUNDS = 2
CAP = 4
GROUP = 4
SLOTS = 8
HALVES = 2
LANES = 128
DUP_LANE = 16
SOURCE_LANE = 20
NOTES = 24
SCALE = 1.0 / math.sqrt(HEAD_DIM)
F32 = jnp.float32
BF16 = jnp.bfloat16
I32 = jnp.int32


def iota(shape, dim):
    return lax.broadcasted_iota(I32, shape, dim)


def hot(condition):
    return jnp.where(condition, 1.0, 0.0).astype(BF16)


def dot(a, b):
    return lax.dot_general(a, b, (((1,), (0,)), ((), ())), preferred_element_type=F32)


def dot_nt(a, b):
    return lax.dot_general(a, b, (((1,), (1,)), ((), ())), preferred_element_type=F32)


def dot_tn(a, b):
    return lax.dot_general(a, b, (((0,), (0,)), ((), ())), preferred_element_type=F32)


def three_parts(x):
    high = x.astype(BF16).astype(F32)
    rest = x - high
    middle = rest.astype(BF16).astype(F32)
    return high, middle, (rest - middle).astype(BF16).astype(F32)


def picked(x, onehot, product):
    rows = x.shape[0]
    stacked = jnp.concatenate(three_parts(x), axis=0).astype(BF16)
    out = product(stacked, onehot)
    return out[:rows] + out[rows : 2 * rows] + out[2 * rows :]


def hot_rows(code, rows=SPAN):
    at = iota((rows, LANES), 0).astype(F32).astype(BF16)
    code = code.astype(F32).astype(BF16)
    pieces = [
        jnp.where(at == code[:, i : i + LANES], jnp.ones_like(at), jnp.zeros_like(at))
        for i in range(0, code.shape[1], LANES)
    ]
    return jnp.concatenate(pieces, axis=1)


def pack_kernel(n, pos_ref, held_ref, send_ref, slots_ref):
    tokens = held_ref.shape[0]
    width = held_ref.shape[1] // 4
    heads = width // HEAD_DIM
    quarters = pos_ref.shape[0] // ROUNDS
    tall = n // GROUP * SLOTS
    before = hot(iota((tokens, tokens), 0) < iota((tokens, tokens), 1))
    main = [[], []]
    edge = []
    notes = []
    slots = []
    all_places = [
        jnp.concatenate(
            [pos_ref[x * ROUNDS + turn : x * ROUNDS + turn + 1, :] for x in range(quarters)], axis=1
        )
        for turn in range(ROUNDS)
    ]
    lane = iota((LANES, tokens), 0)
    for turn in range(ROUNDS):
        places = all_places[turn]
        other = all_places[1 - turn]
        span = places >> 8
        inner = span & 3
        member = hot_rows(span, n)
        earlier = dot(member, before)
        rank = jnp.sum(member.astype(F32) * earlier, axis=0, keepdims=True).astype(I32)
        slots.append(span * CAP + rank)
        row = (span >> 2) * SLOTS + rank
        for half in range(HALVES):
            here = (inner >> 1) == half
            main[half].append(hot_rows(jnp.where(here, row + (inner & 1) * CAP, -1)))
        last = (span & 7) == 7
        first = (((span + 1) & (n - 1)) >> 2) * SLOTS + rank
        edge.append([hot_rows(jnp.where(last, first + i * SLOTS, -1)) for i in range(2)])
        landing = (places & 255) + 1
        values = jnp.where(lane == inner * 4, landing, 0)
        values = jnp.where(lane == inner * 4 + 1, other >> 7, values)
        values = jnp.where(lane == inner * 4 + 2, other & 127, values)
        note = dot_nt(hot_rows(row + CAP), values.astype(F32).astype(BF16))
        values = jnp.where(lane == DUP_LANE, landing, 0).astype(F32).astype(BF16)
        both = [hot_rows(jnp.where(last, first + i * SLOTS + CAP, -1)) for i in range(2)]
        notes.append(note + dot_nt(both[0] + both[1], values))
    slots_ref[...] = jnp.concatenate(slots + [jnp.zeros((8 - ROUNDS, tokens), I32)], axis=0)
    chosen = jnp.concatenate(main[0] + main[1], axis=0)

    def store(column, part):
        for head in range(heads):
            rows = slice(head * ROUNDS * tall, (head + 1) * ROUNDS * tall)
            send_ref[rows, column * HEAD_DIM : (column + 1) * HEAD_DIM] = part[
                :, head * HEAD_DIM : (head + 1) * HEAD_DIM
            ].astype(BF16)

    both = ROUNDS * tall
    for unit in range(4):
        part = dot(chosen, held_ref[:, unit * width : (unit + 1) * width])
        for half in range(HALVES):
            store(half * 4 + unit, part[half * both : (half + 1) * both])
    extra = dot(jnp.concatenate([edge[0][0], edge[1][0]], axis=0), held_ref[:, 2 * width : 3 * width])
    extra = extra + dot(
        jnp.concatenate([edge[0][1], edge[1][1]], axis=0), held_ref[:, 3 * width :]
    )
    notes = jnp.concatenate(notes, axis=0)
    store(HALVES * 4, extra + jnp.concatenate([notes] * heads, axis=1))


def unpack_kernel(n, me_ref, recv_ref, rows_ref, dup_ref, pair_ref, head_ref, info_ref):
    flat = n * SLOTS
    wide = 4 * HEAD_DIM
    odd = (me_ref[0] & 1) == 1
    extra = recv_ref[:, HALVES * wide :]
    at = iota((flat, LANES), 0)
    lane = iota((flat, LANES), 1)
    notes = extra.astype(F32)
    notes = jnp.where((at & 7) < CAP, pltpu.roll(notes, flat - CAP, 0), notes)
    notes = jnp.where(lane == SOURCE_LANE, (at >> 3).astype(F32), notes)
    notes = jnp.where(lane == SOURCE_LANE + 1, (at & 7).astype(F32), notes).astype(BF16)
    by_slot = dot_nt(hot(iota((NOTES, LANES), 0) == iota((NOTES, LANES), 1)), notes).astype(I32)
    upper = (iota((1, flat), 1) & 7) >= CAP
    for half in range(HALVES):
        here = slice(half * 2 * SPAN, (half + 1) * 2 * SPAN)
        chosen = []
        for i in range(2):
            row = (half * 2 + i) * 4
            chosen.append(hot_rows(jnp.where(upper == (i == 1), by_slot[row : row + 1] - 1, -1)))
        chosen = jnp.concatenate(chosen, axis=0)
        rows = dot(chosen, recv_ref[:, half * wide : (half + 1) * wide]).astype(BF16)
        rows_ref[here, :] = rows
        by_place = jnp.transpose(dot(chosen, notes))[:NOTES]
        row = half * 8
        away = [
            jnp.concatenate(
                [by_place[row + i : row + i + 1, :SPAN], by_place[row + i + 4 : row + i + 5, SPAN:]],
                axis=1,
            )
            for i in (1, 2)
        ]
        info = jnp.concatenate(
            away
            + [by_place[SOURCE_LANE : SOURCE_LANE + 2], jnp.zeros((4, 2 * SPAN), F32)],
            axis=0,
        )
        info_ref[:, here] = info
        if half == 0:
            head_ref[:SPAN, :] = rows[:SPAN, : 2 * HEAD_DIM]
            head_ref[SPAN:, :] = jnp.concatenate(
                [info[:, :SPAN], jnp.zeros((8, SPAN), F32)], axis=0
            ).astype(BF16)
    chosen = hot_rows(jnp.where(upper, -1, by_slot[DUP_LANE : DUP_LANE + 1] - 1))
    dup = dot(chosen, extra)
    dup_ref[...] = dup.astype(BF16)
    dup = jnp.concatenate([dup, jnp.zeros_like(dup)], axis=1)
    last = rows_ref[(GROUP - 1) * SPAN :, 2 * HEAD_DIM :].astype(F32)
    pair_ref[...] = jnp.where(odd, dup, last).astype(BF16)


def before_group(odd, dup_ref, pair_ref):
    k_even, v_even = pair_ref[:SPAN, :HEAD_DIM], pair_ref[:SPAN, HEAD_DIM:]
    k_front = jnp.where(odd, k_even.astype(F32), dup_ref[...].astype(F32))
    v_front = jnp.where(odd, v_even.astype(F32), pair_ref[SPAN:, :HEAD_DIM].astype(F32))
    return k_front.astype(BF16), v_front.astype(BF16)


def unit_of(ref, span, unit):
    return ref[span * SPAN : (span + 1) * SPAN, unit * HEAD_DIM : (unit + 1) * HEAD_DIM]


def key_set(rows_ref, front, span):
    if span == 0:
        return [
            jnp.concatenate([front[i], unit_of(rows_ref, 0, 2 + i)], axis=0) for i in range(2)
        ]
    rows = slice((span - 1) * SPAN, (span + 1) * SPAN)
    return [rows_ref[rows, i * HEAD_DIM : (i + 1) * HEAD_DIM] for i in (2, 3)]


def forward_kernel(me_ref, rows_ref, dup_ref, pair_ref, table_ref, stats_ref, tile_ref):
    front = before_group((me_ref[0] & 1) == 1, dup_ref, pair_ref)
    for span in range(GROUP):
        q, g = unit_of(rows_ref, span, 0), unit_of(rows_ref, span, 1)
        k, v = key_set(rows_ref, front, span)
        score = dot_nt(k, q) * SCALE
        highest = jnp.max(score, axis=0, keepdims=True)
        raised = jnp.exp(score - highest)
        total = jnp.sum(raised, axis=0, keepdims=True)
        mixed = jnp.sum(raised * dot_nt(v, g), axis=0, keepdims=True)
        here = slice(span * SPAN, (span + 1) * SPAN)
        log_total = highest + jnp.log(total)
        high = log_total.astype(BF16).astype(F32)
        rows = (high, log_total - high, mixed / total)
        for kind, row in enumerate(rows):
            for i in range(2):
                at = kind * 2 * GROUP + span * 2 + i
                tile_ref[at : at + 1, :] = row[:, i * LANES : (i + 1) * LANES]
        stats_ref[0:1, here] = log_total
        stats_ref[1:2, here] = rows[2]
    stats_ref[2:, :] = jnp.zeros((6, GROUP * SPAN), F32)
    table_ref[...] = jnp.broadcast_to(tile_ref[...].astype(BF16)[None], table_ref.shape)


def backward_kernel(
    n,
    me_ref,
    rows_ref,
    dup_ref,
    pair_ref,
    behind_ref,
    info_ref,
    stats_ref,
    table_ref,
    send_ref,
    grads_ref,
    turned_ref,
):
    flat = n * SLOTS
    groups = n // GROUP
    me = me_ref[0]
    turn = (me >> 5) & 1
    group = (me + 1) & (groups - 1)
    behind_info = behind_ref[SPAN : SPAN + 8, :].astype(F32)
    far = jnp.concatenate([info_ref[0:1, :], behind_info[0:1]], axis=1).astype(I32)
    near = jnp.concatenate([info_ref[1:2, :], behind_info[1:2]], axis=1).astype(I32)
    chosen = hot_rows(far)
    keep = iota((LANES, far.shape[1]), 0) == near

    there = table_ref[pl.ds(pl.multiple_of((1 - turn) * groups, groups), groups)].astype(F32)
    there = [
        jnp.transpose(there[:, kind * 8 : (kind + 1) * 8, :].reshape(groups * 8, LANES))
        for kind in range(3)
    ]
    found = dot(jnp.concatenate(there, axis=0).astype(BF16), chosen)
    other = [
        jnp.sum(jnp.where(keep, values, 0.0), axis=0, keepdims=True)
        for values in (found[:LANES] + found[LANES : 2 * LANES], found[2 * LANES :])
    ]
    tile = table_ref[turn * groups + group].astype(F32)
    tiles = (tile[0:8] + tile[8:16], tile[16:24])
    own = [
        jnp.concatenate([stats_ref[kind : kind + 1, :], tiles[kind][0:1], tiles[kind][1:2]], axis=1)
        for kind in range(2)
    ]
    highest = jnp.maximum(own[0], other[0])
    raised = jnp.exp(own[0] - highest)
    raised_other = jnp.exp(other[0] - highest)
    total = raised + raised_other
    shares = raised / total
    means = (raised * own[1] + raised_other * other[1]) / total

    def graded(keys, vals, queries, grads, log_total, share, mean):
        weighted = jnp.exp(dot_nt(keys, queries) * SCALE - log_total) * share
        grad_score = weighted * ((dot_nt(vals, grads) - mean) * SCALE)
        return weighted.astype(BF16), grad_score.astype(BF16)

    def put(span, unit, grad):
        grads_ref[span * SPAN : (span + 1) * SPAN, unit * HEAD_DIM : (unit + 1) * HEAD_DIM] = (
            grad.astype(BF16)
        )

    front = before_group((me & 1) == 1, dup_ref, pair_ref)
    keys = jnp.concatenate([front[0], rows_ref[:, 2 * HEAD_DIM : 3 * HEAD_DIM]], axis=0)
    keys = jnp.transpose(keys)
    grad_k = None
    grad_v = None
    for span in range(GROUP):
        q, g = unit_of(rows_ref, span, 0), unit_of(rows_ref, span, 1)
        k, v = key_set(rows_ref, front, span)
        here = slice(span * SPAN, (span + 1) * SPAN)
        weight, scaled = graded(k, v, q, g, own[0][:, here], shares[:, here], means[:, here])
        turned_ref[:, here] = dot(keys[:, span * SPAN : (span + 2) * SPAN], scaled).astype(BF16)
        part_k = dot(scaled, q)
        part_v = dot(weight, g)
        if span > 0:
            put(span - 1, 0, grad_k + part_k[:SPAN])
            put(span - 1, 1, grad_v + part_v[:SPAN])
        grad_k = part_k[SPAN:]
        grad_v = part_v[SPAN:]
    here = slice(GROUP * SPAN, (GROUP + 1) * SPAN)
    q, g = behind_ref[:SPAN, :HEAD_DIM], behind_ref[:SPAN, HEAD_DIM:]
    k, v = unit_of(rows_ref, GROUP - 1, 2), unit_of(rows_ref, GROUP - 1, 3)
    weight, scaled = graded(k, v, q, g, own[0][:, here], shares[:, here], means[:, here])
    put(GROUP - 1, 0, grad_k + dot(scaled, q))
    put(GROUP - 1, 1, grad_v + dot(weight, g))
    slot = (info_ref[2:3, :] * SLOTS + info_ref[3:4, :]).astype(I32)
    for half in range(HALVES):
        here = slice(half * 2 * SPAN, (half + 1) * 2 * SPAN)
        for start in range(0, flat, SPAN):
            at = slot[:, here]
            across = hot_rows(jnp.where((at >= start) & (at < start + SPAN), at - start, -1))
            grad_kv = dot(across, grads_ref[here, :])
            grads = (
                dot_nt(across, turned_ref[:, here]),
                grad_kv[:, :HEAD_DIM],
                grad_kv[:, HEAD_DIM:],
            )
            devices = slice(start // SLOTS, (start + SPAN) // SLOTS)
            for unit, grad in enumerate(grads):
                rows = slice((half * 3 + unit) * SLOTS, (half * 3 + unit + 1) * SLOTS)
                send_ref[devices, rows, :] = grad.reshape(SPAN // SLOTS, SLOTS, HEAD_DIM).astype(BF16)


def final_kernel(n, slots_ref, ret_ref, dq_ref, dk_ref, dv_ref):
    tall = n // GROUP * SLOTS
    both = ROUNDS * tall
    slots = jnp.transpose(slots_ref[...].astype(F32)).astype(I32)
    at = iota((slots.shape[0], tall), 1)
    chosen = []
    for half in range(HALVES):
        for turn in range(ROUNDS):
            slot = slots[:, turn : turn + 1]
            row = (slot >> 4) * SLOTS + (slot & 7)
            chosen.append(hot(at == jnp.where(((slot >> 3) & 1) == half, row, -1)))
    chosen = [jnp.concatenate(chosen[i * 2 : i * 2 + 2], axis=1) for i in range(HALVES)]
    devices = both // SLOTS
    for head in range(dq_ref.shape[1] // HEAD_DIM):
        for unit, ref in enumerate((dq_ref, dk_ref, dv_ref)):
            total = None
            for half in range(HALVES):
                rows = slice((half * 3 + unit) * SLOTS, (half * 3 + unit + 1) * SLOTS)
                part = ret_ref[head * devices : (head + 1) * devices, rows, :]
                part = dot(chosen[half], part.reshape(both, HEAD_DIM))
                total = part if total is None else total + part
            ref[:, head * HEAD_DIM : (head + 1) * HEAD_DIM] = total.astype(BF16)


def call(kernel, out, name, args, scratch=()):
    where = [pltpu.SMEM if x.shape == (1,) else pltpu.VMEM for x in args]
    return pl.pallas_call(
        kernel,
        out_shape=out,
        in_specs=[pl.BlockSpec(memory_space=space) for space in where],
        scratch_shapes=scratch,
        name=name,
        compiler_params=pltpu.CompilerParams(vmem_limit_bytes=24 * 1024 * 1024),
    )(*args)


def shape(*dims, dtype=BF16):
    return jax.ShapeDtypeStruct(dims, dtype)


def exchanged(block):
    return lax.all_to_all(block, "seq", split_axis=0, concat_axis=0, tiled=True)


def pair_gathered(block):
    n = lax.axis_size("seq")
    groups = [[i, i + 1] for i in range(0, n, 2)]
    return lax.all_gather(block, "seq", axis=0, tiled=True, axis_index_groups=groups)


def head_exchanged(block):
    n = lax.axis_size("seq")
    groups = [list(range(i, i + n // 2)) for i in (0, n // 2)]
    return lax.all_to_all(
        block, "seq", split_axis=0, concat_axis=0, tiled=True, axis_index_groups=groups
    )


def from_next_group(block):
    n = lax.axis_size("seq")
    groups = n // GROUP
    route = [(i // groups * groups + (i + 1) % groups, i) for i in range(n)]
    return lax.ppermute(block, "seq", route)


def body(queries, keys, values, out_grad, sorted_position):
    n = lax.axis_size("seq")
    tokens, width = queries.shape
    flat = n * SLOTS
    places = GROUP * SPAN
    me = lax.axis_index("seq").astype(I32).reshape(1)
    placed = lax.all_gather(sorted_position, "head", axis=0, tiled=True)
    send, slots = call(
        functools.partial(pack_kernel, n),
        (shape(flat, (4 * HALVES + 1) * HEAD_DIM), shape(8, tokens, dtype=I32)),
        "pack",
        (placed, jnp.concatenate([queries, out_grad, keys, values], axis=1)),
    )
    send, me = lax.optimization_barrier((send, me))
    rows, dup, last, first, info = call(
        functools.partial(unpack_kernel, n),
        (
            shape(places, 4 * HEAD_DIM),
            shape(SPAN, HEAD_DIM),
            shape(SPAN, 2 * HEAD_DIM),
            shape(SPAN + 16, 2 * HEAD_DIM),
            shape(8, places, dtype=F32),
        ),
        "unpack",
        (me, exchanged(send)),
    )
    behind = from_next_group(first)
    pair = pair_gathered(last)
    table, stats = call(
        forward_kernel,
        (shape(n // 2, 3 * 2 * GROUP, LANES), shape(8, places, dtype=F32)),
        "forward",
        (me, rows, dup, pair),
        [pltpu.VMEM((3 * 2 * GROUP, LANES), F32)],
    )
    grads = call(
        functools.partial(backward_kernel, n),
        shape(n, 3 * HALVES * SLOTS, HEAD_DIM),
        "backward",
        (me, rows, dup, pair, behind, info, stats, head_exchanged(table)),
        [pltpu.VMEM((places, 2 * HEAD_DIM), BF16), pltpu.VMEM((HEAD_DIM, places), BF16)],
    )
    return call(
        functools.partial(final_kernel, n),
        (shape(tokens, width),) * 3,
        "final",
        (slots, exchanged(grads)),
    )


def solution(mesh):
    in_specs = (
        P("seq", "head"),
        P("seq", "head"),
        P("seq", "head"),
        P("seq", "head"),
        P(None, ("seq", "head")),
    )
    out_specs = (P("seq", "head"), P("seq", "head"), P("seq", "head"))
    return jax.shard_map(body, mesh=mesh, in_specs=in_specs, out_specs=out_specs, check_vma=False)
```

```python
import functools
import math

import jax
import jax.numpy as jnp
from jax import lax
from jax.experimental import pallas as pl
from jax.experimental.pallas import tpu as pltpu
from jax.sharding import PartitionSpec as P

HEAD_DIM = 128
SPAN = 256
ROUNDS = 2
CAP = 4
GROUP = 4
SLOTS = 8
HALVES = 2
LANES = 128
DUP_LANE = 16
SOURCE_LANE = 20
NOTES = 24
SCALE = 1.0 / math.sqrt(HEAD_DIM)
F32 = jnp.float32
BF16 = jnp.bfloat16
I32 = jnp.int32


def iota(shape, dim):
    return lax.broadcasted_iota(I32, shape, dim)


def hot(condition):
    return jnp.where(condition, 1.0, 0.0).astype(BF16)


def dot(a, b):
    return lax.dot_general(a, b, (((1,), (0,)), ((), ())), preferred_element_type=F32)


def dot_nt(a, b):
    return lax.dot_general(a, b, (((1,), (1,)), ((), ())), preferred_element_type=F32)


def dot_tn(a, b):
    return lax.dot_general(a, b, (((0,), (0,)), ((), ())), preferred_element_type=F32)


def three_parts(x):
    high = x.astype(BF16).astype(F32)
    rest = x - high
    middle = rest.astype(BF16).astype(F32)
    return high, middle, (rest - middle).astype(BF16).astype(F32)


def picked(x, onehot, product):
    rows = x.shape[0]
    stacked = jnp.concatenate(three_parts(x), axis=0).astype(BF16)
    out = product(stacked, onehot)
    return out[:rows] + out[rows : 2 * rows] + out[2 * rows :]


def hot_rows(code, rows=SPAN):
    at = iota((rows, LANES), 0).astype(F32).astype(BF16)
    code = code.astype(F32).astype(BF16)
    pieces = [
        jnp.where(at == code[:, i : i + LANES], jnp.ones_like(at), jnp.zeros_like(at))
        for i in range(0, code.shape[1], LANES)
    ]
    return jnp.concatenate(pieces, axis=1)


def pack_kernel(n, pos_ref, held_ref, send_ref, slots_ref):
    tokens = held_ref.shape[0]
    width = held_ref.shape[1] // 4
    heads = width // HEAD_DIM
    quarters = pos_ref.shape[0] // ROUNDS
    tall = n // GROUP * SLOTS
    before = hot(iota((tokens, tokens), 0) < iota((tokens, tokens), 1))
    main = [[], []]
    edge = []
    notes = []
    slots = []
    all_places = [
        jnp.concatenate(
            [pos_ref[x * ROUNDS + turn : x * ROUNDS + turn + 1, :] for x in range(quarters)], axis=1
        )
        for turn in range(ROUNDS)
    ]
    lane = iota((LANES, tokens), 0)
    for turn in range(ROUNDS):
        places = all_places[turn]
        other = all_places[1 - turn]
        span = places >> 8
        inner = span & 3
        member = hot_rows(span, n)
        earlier = dot(member, before)
        rank = jnp.sum(member.astype(F32) * earlier, axis=0, keepdims=True).astype(I32)
        slots.append(span * CAP + rank)
        row = (span >> 2) * SLOTS + rank
        for half in range(HALVES):
            here = (inner >> 1) == half
            main[half].append(hot_rows(jnp.where(here, row + (inner & 1) * CAP, -1)))
        last = (span & 7) == 7
        first = (((span + 1) & (n - 1)) >> 2) * SLOTS + rank
        edge.append([hot_rows(jnp.where(last, first + i * SLOTS, -1)) for i in range(2)])
        landing = (places & 255) + 1
        values = jnp.where(lane == inner * 4, landing, 0)
        values = jnp.where(lane == inner * 4 + 1, other >> 7, values)
        values = jnp.where(lane == inner * 4 + 2, other & 127, values)
        note = dot_nt(hot_rows(row + CAP), values.astype(F32).astype(BF16))
        values = jnp.where(lane == DUP_LANE, landing, 0).astype(F32).astype(BF16)
        both = [hot_rows(jnp.where(last, first + i * SLOTS + CAP, -1)) for i in range(2)]
        notes.append(note + dot_nt(both[0] + both[1], values))
    slots_ref[...] = jnp.concatenate(slots + [jnp.zeros((8 - ROUNDS, tokens), I32)], axis=0)
    chosen = jnp.concatenate(main[0] + main[1], axis=0)

    def store(column, part):
        for head in range(heads):
            rows = slice(head * ROUNDS * tall, (head + 1) * ROUNDS * tall)
            send_ref[rows, column * HEAD_DIM : (column + 1) * HEAD_DIM] = part[
                :, head * HEAD_DIM : (head + 1) * HEAD_DIM
            ].astype(BF16)

    both = ROUNDS * tall
    for unit in range(4):
        part = dot(chosen, held_ref[:, unit * width : (unit + 1) * width])
        for half in range(HALVES):
            store(half * 4 + unit, part[half * both : (half + 1) * both])
    extra = dot(jnp.concatenate([edge[0][0], edge[1][0]], axis=0), held_ref[:, 2 * width : 3 * width])
    extra = extra + dot(
        jnp.concatenate([edge[0][1], edge[1][1]], axis=0), held_ref[:, 3 * width :]
    )
    notes = jnp.concatenate(notes, axis=0)
    store(HALVES * 4, extra + jnp.concatenate([notes] * heads, axis=1))


def unpack_kernel(n, me_ref, recv_ref, rows_ref, dup_ref, pair_ref, head_ref, info_ref):
    flat = n * SLOTS
    wide = 4 * HEAD_DIM
    odd = (me_ref[0] & 1) == 1
    extra = recv_ref[:, HALVES * wide :]
    at = iota((flat, LANES), 0)
    lane = iota((flat, LANES), 1)
    notes = extra.astype(F32)
    notes = jnp.where((at & 7) < CAP, pltpu.roll(notes, flat - CAP, 0), notes)
    notes = jnp.where(lane == SOURCE_LANE, (at >> 3).astype(F32), notes)
    notes = jnp.where(lane == SOURCE_LANE + 1, (at & 7).astype(F32), notes).astype(BF16)
    by_slot = dot_nt(hot(iota((NOTES, LANES), 0) == iota((NOTES, LANES), 1)), notes).astype(I32)
    upper = (iota((1, flat), 1) & 7) >= CAP
    for half in range(HALVES):
        here = slice(half * 2 * SPAN, (half + 1) * 2 * SPAN)
        chosen = []
        for i in range(2):
            row = (half * 2 + i) * 4
            chosen.append(hot_rows(jnp.where(upper == (i == 1), by_slot[row : row + 1] - 1, -1)))
        chosen = jnp.concatenate(chosen, axis=0)
        rows = dot(chosen, recv_ref[:, half * wide : (half + 1) * wide]).astype(BF16)
        rows_ref[here, :] = rows
        by_place = jnp.transpose(dot(chosen, notes))[:NOTES]
        row = half * 8
        away = [
            jnp.concatenate(
                [by_place[row + i : row + i + 1, :SPAN], by_place[row + i + 4 : row + i + 5, SPAN:]],
                axis=1,
            )
            for i in (1, 2)
        ]
        info = jnp.concatenate(
            away
            + [by_place[SOURCE_LANE : SOURCE_LANE + 2], jnp.zeros((4, 2 * SPAN), F32)],
            axis=0,
        )
        info_ref[:, here] = info
        if half == 0:
            head_ref[:SPAN, :] = rows[:SPAN, : 2 * HEAD_DIM]
            head_ref[SPAN:, :] = jnp.concatenate(
                [info[:, :SPAN], jnp.zeros((8, SPAN), F32)], axis=0
            ).astype(BF16)
    chosen = hot_rows(jnp.where(upper, -1, by_slot[DUP_LANE : DUP_LANE + 1] - 1))
    dup = dot(chosen, extra)
    dup_ref[...] = dup.astype(BF16)
    dup = jnp.concatenate([dup, jnp.zeros_like(dup)], axis=1)
    last = rows_ref[(GROUP - 1) * SPAN :, 2 * HEAD_DIM :].astype(F32)
    pair_ref[...] = jnp.where(odd, dup, last).astype(BF16)


def before_group(odd, dup_ref, pair_ref):
    k_even, v_even = pair_ref[:SPAN, :HEAD_DIM], pair_ref[:SPAN, HEAD_DIM:]
    k_front = jnp.where(odd, k_even.astype(F32), dup_ref[...].astype(F32))
    v_front = jnp.where(odd, v_even.astype(F32), pair_ref[SPAN:, :HEAD_DIM].astype(F32))
    return k_front.astype(BF16), v_front.astype(BF16)


def unit_of(ref, span, unit):
    return ref[span * SPAN : (span + 1) * SPAN, unit * HEAD_DIM : (unit + 1) * HEAD_DIM]


def key_set(rows_ref, front, span):
    if span == 0:
        return [
            jnp.concatenate([front[i], unit_of(rows_ref, 0, 2 + i)], axis=0) for i in range(2)
        ]
    rows = slice((span - 1) * SPAN, (span + 1) * SPAN)
    return [rows_ref[rows, i * HEAD_DIM : (i + 1) * HEAD_DIM] for i in (2, 3)]


def forward_kernel(me_ref, rows_ref, dup_ref, pair_ref, table_ref, stats_ref, tile_ref):
    front = before_group((me_ref[0] & 1) == 1, dup_ref, pair_ref)
    for span in range(GROUP):
        q, g = unit_of(rows_ref, span, 0), unit_of(rows_ref, span, 1)
        k, v = key_set(rows_ref, front, span)
        score = dot_nt(k, q) * SCALE
        highest = jnp.max(score, axis=0, keepdims=True)
        raised = jnp.exp(score - highest)
        total = jnp.sum(raised, axis=0, keepdims=True)
        mixed = jnp.sum(raised * dot_nt(v, g), axis=0, keepdims=True)
        here = slice(span * SPAN, (span + 1) * SPAN)
        log_total = highest + jnp.log(total)
        high = log_total.astype(BF16).astype(F32)
        rows = (high, log_total - high, mixed / total)
        for kind, row in enumerate(rows):
            for i in range(2):
                at = kind * 2 * GROUP + span * 2 + i
                tile_ref[at : at + 1, :] = row[:, i * LANES : (i + 1) * LANES]
        stats_ref[0:1, here] = log_total
        stats_ref[1:2, here] = rows[2]
    stats_ref[2:, :] = jnp.zeros((6, GROUP * SPAN), F32)
    table_ref[...] = jnp.broadcast_to(tile_ref[...].astype(BF16)[None], table_ref.shape)


def backward_kernel(
    n,
    me_ref,
    rows_ref,
    dup_ref,
    pair_ref,
    behind_ref,
    info_ref,
    stats_ref,
    table_ref,
    send_ref,
    grads_ref,
    turned_ref,
):
    flat = n * SLOTS
    groups = n // GROUP
    me = me_ref[0]
    turn = (me >> 5) & 1
    group = (me + 1) & (groups - 1)
    behind_info = behind_ref[SPAN : SPAN + 8, :].astype(F32)
    far = jnp.concatenate([info_ref[0:1, :], behind_info[0:1]], axis=1).astype(I32)
    near = jnp.concatenate([info_ref[1:2, :], behind_info[1:2]], axis=1).astype(I32)
    chosen = hot_rows(far)
    keep = iota((LANES, far.shape[1]), 0) == near

    there = table_ref[pl.ds(pl.multiple_of((1 - turn) * groups, groups), groups)].astype(F32)
    there = [
        jnp.transpose(there[:, kind * 8 : (kind + 1) * 8, :].reshape(groups * 8, LANES))
        for kind in range(3)
    ]
    found = dot(jnp.concatenate(there, axis=0).astype(BF16), chosen)
    other = [
        jnp.sum(jnp.where(keep, values, 0.0), axis=0, keepdims=True)
        for values in (found[:LANES] + found[LANES : 2 * LANES], found[2 * LANES :])
    ]
    tile = table_ref[turn * groups + group].astype(F32)
    tiles = (tile[0:8] + tile[8:16], tile[16:24])
    own = [
        jnp.concatenate([stats_ref[kind : kind + 1, :], tiles[kind][0:1], tiles[kind][1:2]], axis=1)
        for kind in range(2)
    ]
    highest = jnp.maximum(own[0], other[0])
    raised = jnp.exp(own[0] - highest)
    raised_other = jnp.exp(other[0] - highest)
    total = raised + raised_other
    shares = raised / total
    means = (raised * own[1] + raised_other * other[1]) / total

    def graded(keys, vals, queries, grads, log_total, share, mean):
        weighted = jnp.exp(dot_nt(keys, queries) * SCALE - log_total) * share
        grad_score = weighted * ((dot_nt(vals, grads) - mean) * SCALE)
        return weighted.astype(BF16), grad_score.astype(BF16)

    def put(span, unit, grad):
        grads_ref[span * SPAN : (span + 1) * SPAN, unit * HEAD_DIM : (unit + 1) * HEAD_DIM] = (
            grad.astype(BF16)
        )

    front = before_group((me & 1) == 1, dup_ref, pair_ref)
    keys = jnp.concatenate([front[0], rows_ref[:, 2 * HEAD_DIM : 3 * HEAD_DIM]], axis=0)
    keys = jnp.transpose(keys)
    grad_k = None
    grad_v = None
    for span in range(GROUP):
        q, g = unit_of(rows_ref, span, 0), unit_of(rows_ref, span, 1)
        k, v = key_set(rows_ref, front, span)
        here = slice(span * SPAN, (span + 1) * SPAN)
        weight, scaled = graded(k, v, q, g, own[0][:, here], shares[:, here], means[:, here])
        turned_ref[:, here] = dot(keys[:, span * SPAN : (span + 2) * SPAN], scaled).astype(BF16)
        part_k = dot(scaled, q)
        part_v = dot(weight, g)
        if span > 0:
            put(span - 1, 0, grad_k + part_k[:SPAN])
            put(span - 1, 1, grad_v + part_v[:SPAN])
        grad_k = part_k[SPAN:]
        grad_v = part_v[SPAN:]
    here = slice(GROUP * SPAN, (GROUP + 1) * SPAN)
    q, g = behind_ref[:SPAN, :HEAD_DIM], behind_ref[:SPAN, HEAD_DIM:]
    k, v = unit_of(rows_ref, GROUP - 1, 2), unit_of(rows_ref, GROUP - 1, 3)
    weight, scaled = graded(k, v, q, g, own[0][:, here], shares[:, here], means[:, here])
    put(GROUP - 1, 0, grad_k + dot(scaled, q))
    put(GROUP - 1, 1, grad_v + dot(weight, g))
    wide = 3 * HEAD_DIM
    slot = (info_ref[2:3, :] * SLOTS + info_ref[3:4, :]).astype(I32)
    for half in range(HALVES):
        here = slice(half * 2 * SPAN, (half + 1) * 2 * SPAN)
        for start in range(0, flat, SPAN):
            at = slot[:, here]
            across = hot_rows(jnp.where((at >= start) & (at < start + SPAN), at - start, -1))
            rows = slice(start, start + SPAN)
            middle = half * wide + HEAD_DIM
            send_ref[rows, half * wide : middle] = dot_nt(across, turned_ref[:, here]).astype(BF16)
            send_ref[rows, middle : (half + 1) * wide] = dot(across, grads_ref[here, :]).astype(BF16)


def final_kernel(n, slots_ref, ret_ref, dq_ref, dk_ref, dv_ref):
    tall = n // GROUP * SLOTS
    both = ROUNDS * tall
    wide = 3 * HEAD_DIM
    slots = jnp.transpose(slots_ref[...].astype(F32)).astype(I32)
    at = iota((slots.shape[0], tall), 1)
    chosen = []
    for half in range(HALVES):
        for turn in range(ROUNDS):
            slot = slots[:, turn : turn + 1]
            row = (slot >> 4) * SLOTS + (slot & 7)
            chosen.append(hot(at == jnp.where(((slot >> 3) & 1) == half, row, -1)))
    chosen = [jnp.concatenate(chosen[i * 2 : i * 2 + 2], axis=1) for i in range(HALVES)]
    for head in range(dq_ref.shape[1] // HEAD_DIM):
        rows = slice(head * both, (head + 1) * both)
        total = dot(chosen[0], ret_ref[rows, :wide]) + dot(chosen[1], ret_ref[rows, wide:])
        for unit, ref in enumerate((dq_ref, dk_ref, dv_ref)):
            ref[:, head * HEAD_DIM : (head + 1) * HEAD_DIM] = total[
                :, unit * HEAD_DIM : (unit + 1) * HEAD_DIM
            ].astype(BF16)


def call(kernel, out, name, args, scratch=()):
    where = [pltpu.SMEM if x.shape == (1,) else pltpu.VMEM for x in args]
    return pl.pallas_call(
        kernel,
        out_shape=out,
        in_specs=[pl.BlockSpec(memory_space=space) for space in where],
        scratch_shapes=scratch,
        name=name,
        compiler_params=pltpu.CompilerParams(vmem_limit_bytes=24 * 1024 * 1024),
    )(*args)


def shape(*dims, dtype=BF16):
    return jax.ShapeDtypeStruct(dims, dtype)


def exchanged(block):
    return lax.all_to_all(block, "seq", split_axis=0, concat_axis=0, tiled=True)


def pair_gathered(block):
    n = lax.axis_size("seq")
    groups = [[i, i + 1] for i in range(0, n, 2)]
    return lax.all_gather(block, "seq", axis=0, tiled=True, axis_index_groups=groups)


def head_exchanged(block):
    n = lax.axis_size("seq")
    groups = [list(range(i, i + n // 2)) for i in (0, n // 2)]
    return lax.all_to_all(
        block, "seq", split_axis=0, concat_axis=0, tiled=True, axis_index_groups=groups
    )


def from_next_group(block):
    n = lax.axis_size("seq")
    groups = n // GROUP
    route = [(i // groups * groups + (i + 1) % groups, i) for i in range(n)]
    return lax.ppermute(block, "seq", route)


def body(queries, keys, values, out_grad, sorted_position):
    n = lax.axis_size("seq")
    tokens, width = queries.shape
    flat = n * SLOTS
    places = GROUP * SPAN
    me = lax.axis_index("seq").astype(I32).reshape(1)
    placed = lax.all_gather(sorted_position, "head", axis=0, tiled=True)
    send, slots = call(
        functools.partial(pack_kernel, n),
        (shape(flat, (4 * HALVES + 1) * HEAD_DIM), shape(8, tokens, dtype=I32)),
        "pack",
        (placed, jnp.concatenate([queries, out_grad, keys, values], axis=1)),
    )
    send, me = lax.optimization_barrier((send, me))
    rows, dup, last, first, info = call(
        functools.partial(unpack_kernel, n),
        (
            shape(places, 4 * HEAD_DIM),
            shape(SPAN, HEAD_DIM),
            shape(SPAN, 2 * HEAD_DIM),
            shape(SPAN + 16, 2 * HEAD_DIM),
            shape(8, places, dtype=F32),
        ),
        "unpack",
        (me, exchanged(send)),
    )
    behind = from_next_group(first)
    pair = pair_gathered(last)
    table, stats = call(
        forward_kernel,
        (shape(n // 2, 3 * 2 * GROUP, LANES), shape(8, places, dtype=F32)),
        "forward",
        (me, rows, dup, pair),
        [pltpu.VMEM((3 * 2 * GROUP, LANES), F32)],
    )
    grads = call(
        functools.partial(backward_kernel, n),
        shape(flat, 3 * HALVES * HEAD_DIM),
        "backward",
        (me, rows, dup, pair, behind, info, stats, head_exchanged(table)),
        [pltpu.VMEM((places, 2 * HEAD_DIM), BF16), pltpu.VMEM((HEAD_DIM, places), BF16)],
    )
    return call(
        functools.partial(final_kernel, n),
        (shape(tokens, width),) * 3,
        "final",
        (slots, exchanged(grads)),
    )


def solution(mesh):
    in_specs = (
        P("seq", "head"),
        P("seq", "head"),
        P("seq", "head"),
        P("seq", "head"),
        P(None, ("seq", "head")),
    )
    out_specs = (P("seq", "head"), P("seq", "head"), P("seq", "head"))
    return jax.shard_map(body, mesh=mesh, in_specs=in_specs, out_specs=out_specs, check_vma=False)
```
